128 devices in a mesh: grp: 2 (over core), ep: 32 (over z_lo, x, y), mp: 2 (over z_hi).
Axes of the slice: x: 4, y: 4, z: 4 (z_hi: 2, z_lo: 2; z = z_hi * 2 + z_lo), core: 2. Of those that a mesh axis runs over, the one named last changes fastest.
Arguments:
- teacher_rows: bfloat16 [16384, 2048], P(('grp', 'ep')), may hold values from -6 to 6
- expert_ids: int32 [16384, 2], P(('grp', 'ep')), may hold values from 0 to 31, all different within a row; in each aligned block of 256 rows (0 to 255, 256 to 511, ...) at most 32 rows name the same one
- router: bfloat16 [2048, 32], replicated, may hold values from -0.5 to 0.5
- teacher_up: bfloat16 [32, 2048, 4096], P('ep', None, 'mp'), may hold values from -0.125 to 0.125
- teacher_down: bfloat16 [32, 4096, 2048], P('ep', 'mp'), may hold values from -0.1875 to 0.1875
- student_experts: bfloat16 [2048, 1024], replicated, may hold values from -0.25 to 0.25
- student_gates: bfloat16 [2048, 48], replicated, may hold values from -0.5 to 0.5
- tower_in: bfloat16 [6, 128, 256], replicated, may hold values from -1 to 1
- tower_out: bfloat16 [6, 256], replicated, may hold values from -0.75 to 0.75
- soft_labels: float32 [16384, 6], P(('grp', 'ep', 'mp')), may hold values from 0.02 to 0.98
- label_masks: int32 [16384, 6], P(('grp', 'ep', 'mp')), may hold values 0 or 1
Outputs:
- grad_experts: float32 [2048, 1024], replicated
- grad_gates: float32 [2048, 48], replicated
- grad_tower_in: float32 [6, 128, 256], replicated
- grad_tower_out: float32 [6, 256], replicated
The draws below stay inside these ranges and needn't reach their ends.
Inputs may be any that keep to these rules, and one draw needn't show every extreme that they name: `expert_ids`: each sample names 2 different experts. Within each block of 256 consecutive samples no expert is named by more than 32 samples, and in every draw some block names some expert exactly 32 times.
All inputs are finite; a program needn't handle non-finite values. No bound on the sum of `label_masks` on one device may be relied on, other than what follows from the above.
Results may differ from the reference program's by a relative error of at most 0.023.
The reference program's roundings to bfloat16 on the way count: a program that leaves them out, or rounds other values in their place, can miss the bound.
Values may be sent and summed in bfloat16 or wider, within the bound.
No kernel may reach another device: no remote copies, remote signals or barrier semaphores. Data moves between devices by JAX's collectives and lax.ppermute only.
A program may use at most 128 MiB of HBM per device.

```python
import math
import jax
import jax.numpy as jnp
import numpy as np
from jax import lax

D = 2048
EH = 4096
TOP = 2
NE = 8
SE = 128
TH = 256
TASKS = 6
TOK_DEV = 256
EXPERTS = 32
CAP = 32
TOKENS = 16384
N_MP = 2


def plant(array, key, smallest, high):
    shape = array.shape
    place = [jax.random.randint(jax.random.fold_in(key, axis), (), 0, shape[axis]) for axis in range(len(shape))]
    array = array.at[tuple(place)].set(smallest)
    longest = shape.index(max(shape))
    place[longest] = (place[longest] + 1) % shape[longest]
    return array.at[tuple(place)].set(high)


def steps_of(key, dims, cuts, low, top_value):
    level = 1.0
    for axis_at, blocks in cuts:
        steps = jax.random.uniform(jax.random.fold_in(jax.random.fold_in(key, 6), axis_at), (blocks,), jnp.float32, low / len(cuts), top_value / len(cuts))
        level = level * jnp.repeat(jnp.exp(steps), dims[axis_at] // blocks).reshape((-1,) + (1,) * (len(dims) - 1 - axis_at))
    return level


def deal_out(rng, own, number, rows, amount, top, reach, slope):
    order = jax.random.permutation(rng, amount)
    packed, ordinary = load_shares(amount, rows * top, reach, slope, True), load_shares(amount, rows * top, reach, slope, False)
    places = jnp.arange(amount)

    def named(sizes, offset_by):
        used = int((sizes > 0).sum())
        fixed = max(1, used // 4)
        moved = fixed + (places - fixed + offset_by * (used - fixed)) % max(1, amount - fixed)
        return jnp.zeros((amount,), jnp.int32).at[order[jnp.where(places < fixed, places, moved)]].set(jnp.asarray(sizes, jnp.int32))

    sizes = jnp.where(number % 4 == 0, named(packed, number // 4), named(ordinary, number - number // 4 - 1))
    mixed = jax.random.permutation(jax.random.fold_in(own, 3), amount)
    giver, sink = mixed[0:amount // 2 * 2:2], mixed[1:amount // 2 * 2:2]
    slack = jnp.minimum(sizes[giver] - 1, reach - sizes[sink]) // 2
    slack = jnp.where((giver == order[0]) | (sink == order[0]) | (sizes[sink] == 0), 0, jnp.maximum(slack, 0))
    moved = jax.random.randint(jax.random.fold_in(own, 4), (amount // 2,), 0, 1 << 20) % (slack + 1)
    sizes = sizes.at[giver].add(-moved).at[sink].add(moved)
    items = jnp.searchsorted(jnp.cumsum(sizes), jnp.arange(rows * top), side="right").astype(jnp.int32)
    listing = items.reshape(top, rows).T
    listing = listing[jax.random.permutation(jax.random.fold_in(own, 1), rows)]
    offset_by = jax.random.randint(jax.random.fold_in(own, 2), (rows, 1), 0, top)
    return jnp.take_along_axis(listing, (jnp.arange(top)[None, :] + offset_by) % top, axis=1)


def load_shares(amount, total, reach, lean, full):
    loads = [(1 << 20) // math.isqrt(grade ** lean) + 1 for grade in range(1, amount + 1)]
    largest = reach if full else min(reach, max(-(-total // amount), total * loads[0] // sum(loads)))
    least = 1 if total - largest >= amount - 1 else 0
    counts, spare = [largest] + [least] * (amount - 1), total - largest - least * (amount - 1)
    while spare > 0:
        movable = [i for i in range(1, amount) if counts[i] < largest] or [i for i in range(1, amount) if counts[i] < reach]
        pool, budget = sum([loads[i] for i in movable]), spare
        for i in movable:
            more = min(reach - counts[i], max(1, budget * loads[i] // pool), spare)
            counts[i] = counts[i] + more
            spare = spare - more
    return np.array(counts)


def centred(own_key, extent, width, most, shards=(), held_as=jnp.bfloat16):
    entries = width * jax.random.normal(own_key, extent, jnp.float32)
    if shards:
        entries = entries * steps_of(own_key, extent, shards, -0.22, 0.18)
    return jnp.clip(entries, -most, most).astype(held_as)


def setup_inputs(seed: int = 0) -> dict:
    seeds = jax.random.split(jax.random.key(seed), 12)
    teacher_rows = centred(seeds[0], (TOKENS, D), 1.0, 6.0, ((0, 64),))
    expert_ids_keys = jax.random.split(jax.random.fold_in(seeds[1], 1), TOKENS // TOK_DEV)
    expert_ids_turns = jax.random.permutation(jax.random.fold_in(seeds[1], 3), TOKENS // TOK_DEV)
    expert_ids = jax.vmap(lambda own, number: deal_out(jax.random.fold_in(seeds[1], 2), own, number, TOK_DEV, EXPERTS, TOP, CAP, 2))(expert_ids_keys, expert_ids_turns).reshape((TOKENS, TOP))
    router = centred(seeds[2], (D, EXPERTS), (D // 16) ** -0.5, 0.5)
    teacher_up = centred(seeds[3], (EXPERTS, D, EH), D ** -0.5, 0.125, ((0, 32), (2, 2)))
    teacher_down = centred(seeds[4], (EXPERTS, EH, D), (EH // 4) ** -0.5, 0.1875, ((0, 32), (1, 2)))
    student_experts = centred(seeds[5], (D, NE * SE), (D // 4) ** -0.5, 0.25)
    student_gates = centred(seeds[6], (D, TASKS * NE), (D // 16) ** -0.5, 0.5)
    tower_in = centred(seeds[7], (TASKS, SE, TH), (SE // 4) ** -0.5, 1.0)
    tower_out = centred(seeds[8], (TASKS, TH), (TH // 4) ** -0.5, 0.75)
    soft_labels = jnp.clip(0.02 + 0.96000002 * jax.random.uniform(seeds[9], (TOKENS, TASKS), jnp.float32) ** steps_of(seeds[9], (TOKENS, TASKS), ((0, 128),), -0.2, 0.2), 0.02, 0.98)
    label_masks = plant((jax.random.randint(seeds[10], (TOKENS, TASKS), 0, 4) < 3).astype(jnp.int32), jax.random.fold_in(seeds[10], 1), 0, 1)
    return {"teacher_rows": teacher_rows, "expert_ids": expert_ids, "router": router, "teacher_up": teacher_up, "teacher_down": teacher_down, "student_experts": student_experts, "student_gates": student_gates, "tower_in": tower_in, "tower_out": tower_out, "soft_labels": soft_labels, "label_masks": label_masks}


def student_grads(rows_in, experts_w, gates_w, tower_w, tower_v, soft_labels, label_masks, loss_scale):
    count_rows = rows_in.shape[0]
    task_count, expert_width, tower_width = tower_w.shape
    expert_count = gates_w.shape[1] // task_count
    pre_act = jnp.dot(rows_in, experts_w, preferred_element_type=jnp.float32)
    activation, gelu_back = jax.vjp(jax.nn.gelu, pre_act)
    act_three = activation.reshape(count_rows, expert_count, expert_width)
    gate_logit = jnp.dot(rows_in, gates_w, preferred_element_type=jnp.float32).reshape(count_rows, task_count, expert_count)
    gate_sig = jax.nn.sigmoid(gate_logit)
    gate_sum = lax.optimization_barrier(jnp.sum(gate_sig, -1, keepdims=True))
    gate_share = gate_sig / gate_sum
    mixture = jnp.einsum('ntk,nks->nts', gate_share, act_three).astype(jnp.bfloat16)
    tower_pre = jnp.einsum('nts,tsh->nth', mixture.astype(jnp.float32), tower_w.astype(jnp.float32))
    tower_sig = jax.nn.sigmoid(tower_pre)
    tower_hid = tower_pre * tower_sig
    task_logit = jnp.einsum('nth,th->nt', tower_hid, tower_v.astype(jnp.float32))
    logit_grad = label_masks.astype(jnp.float32) * (jax.nn.sigmoid(task_logit) - soft_labels) * loss_scale
    grad_tower_out = jnp.einsum('nt,nth->th', logit_grad, tower_hid)
    hid_grad = logit_grad[:, :, None] * tower_v.astype(jnp.float32)[None, :, :]
    tower_grad = (hid_grad * tower_sig * (1.0 + tower_pre * (1.0 - tower_sig))).astype(jnp.bfloat16)
    grad_tower_in = jnp.einsum('nts,nth->tsh', mixture.astype(jnp.float32), tower_grad.astype(jnp.float32))
    mixture_grad = jnp.einsum('nth,tsh->nts', tower_grad.astype(jnp.float32), tower_w.astype(jnp.float32))
    act_grad = jnp.einsum('ntk,nts->nks', gate_share, mixture_grad)
    share_grad = jnp.einsum('nts,nks->ntk', mixture_grad, act_three)
    sig_grad = (share_grad - lax.optimization_barrier(jnp.sum(gate_share * share_grad, -1, keepdims=True))) / gate_sum
    gate_grad = (sig_grad * gate_sig * (1.0 - gate_sig)).astype(jnp.bfloat16).reshape(count_rows, task_count * expert_count)
    grad_gates = jnp.einsum('nd,ng->dg', rows_in.astype(jnp.float32), gate_grad.astype(jnp.float32))
    pre_grad = gelu_back(act_grad.reshape(count_rows, expert_count * expert_width))[0].astype(jnp.bfloat16)
    grad_experts = jnp.einsum('nd,nf->df', rows_in.astype(jnp.float32), pre_grad.astype(jnp.float32))
    return (grad_experts, grad_gates, grad_tower_in, grad_tower_out)

def one_expert(operands):
    rows_in, up_proj, down_proj = operands
    inner_act = jax.nn.gelu(jnp.dot(rows_in, up_proj, preferred_element_type=jnp.float32)).astype(jnp.bfloat16)
    part_width = up_proj.shape[1] // N_MP
    summed = jnp.zeros((rows_in.shape[0], down_proj.shape[1]), jnp.float32)
    for part_index in range(N_MP):
        lower = part_index * part_width
        piece = jnp.dot(inner_act[:, lower:lower + part_width], down_proj[lower:lower + part_width], preferred_element_type=jnp.float32)
        rounded = lax.optimization_barrier(piece.astype(jnp.bfloat16))
        summed = summed + rounded.astype(jnp.float32)
    return summed.astype(jnp.bfloat16)

def reference(teacher_rows, expert_ids, router, teacher_up, teacher_down, student_experts, student_gates, tower_in, tower_out, soft_labels, label_masks):
    sources = TOKENS // TOK_DEV
    logits = jnp.dot(teacher_rows, router, preferred_element_type=jnp.float32)
    onehot = (expert_ids[:, :, None] == jnp.arange(EXPERTS, dtype=jnp.int32)[None, None, :]).astype(jnp.int32)
    chosen = lax.optimization_barrier(jnp.sum(logits[:, None, :] * onehot.astype(jnp.float32), -1))
    route_sig = jax.nn.sigmoid(chosen)
    route_weight = route_sig / lax.optimization_barrier(jnp.sum(route_sig, -1, keepdims=True))
    block_hot = onehot.reshape(sources, TOP * TOK_DEV, EXPERTS)
    earlier = jnp.cumsum(block_hot, axis=1) - block_hot
    slot_index = lax.optimization_barrier(jnp.sum(earlier * block_hot, -1)).astype(jnp.int32)
    target = (expert_ids.reshape(sources, TOP * TOK_DEV) * (sources * CAP) + jnp.arange(sources, dtype=jnp.int32)[:, None] * CAP + slot_index).astype(jnp.int32)
    sample_index = (jnp.arange(TOKENS * TOP, dtype=jnp.int32) // TOP).astype(jnp.int32)
    slot_table = jnp.full((EXPERTS * sources * CAP,), TOKENS, jnp.int32).at[target.reshape(-1)].set(sample_index)
    padded = jnp.concatenate([teacher_rows, jnp.zeros((1, D), teacher_rows.dtype)], 0)
    dispatched = padded[slot_table].reshape(EXPERTS, sources * CAP, D)
    expert_out = lax.map(one_expert, (dispatched, teacher_up, teacher_down))
    picked = expert_out.reshape(EXPERTS * sources * CAP, D)[target.reshape(-1)].reshape(TOKENS, TOP, D)
    teacher_out = lax.optimization_barrier(jnp.sum(route_weight[:, :, None] * picked.astype(jnp.float32), 1)).astype(jnp.bfloat16)
    student_in = jnp.roll(teacher_out, TOKENS // 2, axis=0)
    loss_scale = 1.0 / math.sqrt(TOKENS)
    grad_experts, grad_gates, grad_tower_in, grad_tower_out = student_grads(student_in, student_experts, student_gates, tower_in, tower_out, soft_labels, label_masks, loss_scale)
    return (grad_experts, grad_gates, grad_tower_in, grad_tower_out)
```

```python
import math

import jax
import jax.numpy as jnp
from jax import lax
from jax.sharding import PartitionSpec as P

F32 = jnp.float32
BF16 = jnp.bfloat16
SLOT_CHUNKS = 2
CHIPS = ("ep", "mp")


def swap(shard, axis):
    return lax.ppermute(shard, axis, [(0, 1), (1, 0)])


def student_grads(rows_in, experts_w, gates_w, tower_w, tower_v, soft_labels, masks, loss_scale):
    count_rows = rows_in.shape[0]
    task_count, expert_width, tower_width = tower_w.shape
    expert_count = gates_w.shape[1] // task_count
    pre_act = jnp.dot(rows_in, experts_w, preferred_element_type=F32)
    activation, gelu_back = jax.vjp(jax.nn.gelu, pre_act)
    act_three = activation.reshape(count_rows, expert_count, expert_width)
    gate_logit = jnp.dot(rows_in, gates_w, preferred_element_type=F32).reshape(
        count_rows, task_count, expert_count
    )
    gate_sig = jax.nn.sigmoid(gate_logit)
    gate_sum = jnp.sum(gate_sig, -1, keepdims=True)
    gate_share = gate_sig / gate_sum
    mixture = jnp.einsum("ntk,nks->nts", gate_share, act_three).astype(BF16)
    tower_pre = jnp.einsum("nts,tsh->nth", mixture, tower_w, preferred_element_type=F32)
    tower_sig = jax.nn.sigmoid(tower_pre)
    tower_hid = tower_pre * tower_sig
    tower_vec = tower_v.astype(F32)
    task_logit = jnp.einsum("nth,th->nt", tower_hid, tower_vec)
    logit_grad = masks * (jax.nn.sigmoid(task_logit) - soft_labels) * loss_scale
    grad_tower_out = jnp.einsum("nt,nth->th", logit_grad, tower_hid)
    hid_grad = logit_grad[:, :, None] * tower_vec[None, :, :]
    tower_grad = (hid_grad * tower_sig * (1.0 + tower_pre * (1.0 - tower_sig))).astype(BF16)
    grad_tower_in = jnp.einsum("nts,nth->tsh", mixture, tower_grad, preferred_element_type=F32)
    mixture_grad = jnp.einsum("nth,tsh->nts", tower_grad, tower_w, preferred_element_type=F32)
    act_grad = jnp.einsum("ntk,nts->nks", gate_share, mixture_grad)
    share_grad = jnp.einsum("nts,nks->ntk", mixture_grad, act_three)
    sig_grad = (share_grad - jnp.sum(gate_share * share_grad, -1, keepdims=True)) / gate_sum
    gate_grad = (
        (sig_grad * gate_sig * (1.0 - gate_sig))
        .astype(BF16)
        .reshape(count_rows, task_count * expert_count)
    )
    pre_grad = gelu_back(act_grad.reshape(count_rows, expert_count * expert_width))[0].astype(BF16)
    return pre_grad, gate_grad, grad_tower_in, grad_tower_out


def on_device(
    teacher_rows,
    expert_ids,
    router,
    teacher_up,
    teacher_down,
    student_experts,
    student_gates,
    tower_in,
    tower_out,
    soft_labels,
    label_masks,
):
    rows_dev, feature_dim = teacher_rows.shape
    expert_total = lax.axis_size("ep")
    width_parts = lax.axis_size("mp")
    group_index = lax.axis_index("grp")
    chips = expert_total * width_parts
    capacity = 4 * rows_dev // expert_total
    chunk_slots = capacity // SLOT_CHUNKS

    labels = swap(jnp.concatenate([soft_labels, label_masks.astype(F32)], 1), "grp")
    task_count = soft_labels.shape[1]

    experts = jnp.arange(expert_total, dtype=jnp.int32)
    hot = [(expert_ids[:, c : c + 1] == experts[None, :]) for c in range(2)]
    named = (hot[0] | hot[1]).astype(BF16)
    sample = jnp.arange(rows_dev, dtype=jnp.int32)
    before = (sample[None, :] < sample[:, None]).astype(BF16)
    earlier = jnp.dot(before, named, preferred_element_type=F32)
    slots = [jnp.sum(jnp.where(h, earlier, 0.0), 1, keepdims=True).astype(jnp.int32) for h in hot]

    def places(chunk):
        found = []
        for c in range(2):
            local = slots[c] - chunk * chunk_slots
            inside = (local >= 0) & (local < chunk_slots)
            found.append(jnp.where(inside, expert_ids[:, c : c + 1] * chunk_slots + local, -1))
        return found

    lane = jnp.arange(expert_total * chunk_slots, dtype=jnp.int32)[None, :]
    targets = [places(chunk) for chunk in range(SLOT_CHUNKS)]

    received = []
    for first, second in targets:
        pick = ((lane == first) | (lane == second)).astype(BF16)
        outgoing = lax.dot_general(
            pick, teacher_rows, (((0,), (0,)), ((), ())), preferred_element_type=F32
        ).astype(BF16)
        outgoing = outgoing.reshape(expert_total, chunk_slots, feature_dim)
        received.append(lax.all_to_all(outgoing, "ep", split_axis=0, concat_axis=0, tiled=True))

    logits = jnp.dot(teacher_rows, router, preferred_element_type=F32)
    chosen = [jnp.sum(jnp.where(h, logits, 0.0), 1, keepdims=True) for h in hot]
    sigs = [jax.nn.sigmoid(v) for v in chosen]
    weights = [v / (sigs[0] + sigs[1]) for v in sigs]

    up_proj = teacher_up[0]
    down_proj = teacher_down[0]
    mixed = jnp.zeros((rows_dev, feature_dim), F32)
    for chunk in range(SLOT_CHUNKS):
        rows_in = received[chunk].reshape(expert_total * chunk_slots, feature_dim)
        inner = jax.nn.gelu(jnp.dot(rows_in, up_proj, preferred_element_type=F32)).astype(BF16)
        partial = jnp.dot(inner, down_proj, preferred_element_type=F32).astype(BF16)
        returned = lax.all_to_all(
            partial.reshape(expert_total, chunk_slots, feature_dim),
            "ep",
            split_axis=0,
            concat_axis=0,
            tiled=True,
        ).reshape(expert_total * chunk_slots, feature_dim)
        first, second = targets[chunk]
        share = jnp.where(lane == first, weights[0], 0.0) + jnp.where(
            lane == second, weights[1], 0.0
        )
        high = share.astype(BF16)
        low = (share - high.astype(F32)).astype(BF16)
        mixed = mixed + jnp.dot(high, returned, preferred_element_type=F32)
        mixed = mixed + jnp.dot(low, returned, preferred_element_type=F32)
    mixed = mixed.astype(BF16)

    half_rows = rows_dev // width_parts
    part = lax.axis_index("mp")
    kept = lax.dynamic_slice_in_dim(mixed, part * half_rows, half_rows, 0)
    given = lax.dynamic_slice_in_dim(mixed, (1 - part) * half_rows, half_rows, 0)
    own_rows = (kept.astype(F32) + swap(given, "mp").astype(F32)).astype(BF16)
    other_rows = swap(own_rows, "grp")

    sample_total = rows_dev * lax.axis_size("grp") * expert_total
    pre_grad, gate_grad, grad_tower_in, grad_tower_out = student_grads(
        own_rows,
        student_experts,
        student_gates,
        tower_in,
        tower_out,
        labels[:, :task_count],
        labels[:, task_count:],
        1.0 / math.sqrt(sample_total),
    )

    def halves(array, axis):
        size = array.shape[axis] // 2
        mine = lax.dynamic_slice_in_dim(array, group_index * size, size, axis)
        theirs = lax.dynamic_slice_in_dim(array, (1 - group_index) * size, size, axis)
        return mine, theirs

    both_rows = jnp.concatenate([own_rows, other_rows], 0)
    mine, theirs = halves(pre_grad, 1)
    pre_both = jnp.concatenate([mine, swap(theirs, "grp")], 0)
    mine, theirs = halves(gate_grad, 1)
    gate_both = jnp.concatenate([mine, swap(theirs, "grp")], 0)
    contract = (((0,), (0,)), ((), ()))
    main = lax.dot_general(both_rows, pre_both, contract, preferred_element_type=F32).astype(BF16)
    gates = lax.dot_general(gate_both, both_rows, contract, preferred_element_type=F32)
    mine, theirs = halves(grad_tower_in.astype(BF16), 0)
    tower = mine.astype(F32) + swap(theirs, "grp").astype(F32)
    mine, theirs = halves(grad_tower_out.astype(BF16), 0)
    vector = mine.astype(F32) + swap(theirs, "grp").astype(F32)

    width = main.shape[1]
    tower_rows = tower.reshape(-1, tower.shape[2])
    tower_half = tower_rows.shape[0] // 2
    tower_block = jnp.concatenate([tower_rows[:tower_half], tower_rows[tower_half:]], 1)
    gate_block = gates.reshape(-1, width)
    vector_flat = vector.reshape(-1)
    vector_rows = -(-vector_flat.shape[0] // width)
    vector_block = jnp.pad(vector_flat, (0, vector_rows * width - vector_flat.shape[0]))
    small = jnp.concatenate(
        [tower_block, gate_block, vector_block.reshape(vector_rows, width)], 0
    ).astype(BF16)
    small_each = -(-small.shape[0] // (8 * chips)) * 8
    small = jnp.pad(small, ((0, small_each * chips - small.shape[0]), (0, 0)))
    main_each = main.shape[0] // chips
    packed = jnp.concatenate(
        [main.reshape(chips, main_each, width), small.reshape(chips, small_each, width)], 1
    )

    parts = lax.all_to_all(packed, CHIPS, split_axis=0, concat_axis=0, tiled=True)
    total = jnp.sum(parts.astype(F32), 0).astype(BF16)
    spread = jnp.broadcast_to(total[None], packed.shape)
    own_half = lax.all_to_all(spread, CHIPS, split_axis=0, concat_axis=0, tiled=True)
    other_half = swap(own_half, "grp")
    low_half = jnp.where(group_index == 0, own_half, other_half)
    high_half = jnp.where(group_index == 0, other_half, own_half)

    main_halves, tower_halves, gate_halves, vector_halves = [], [], [], []
    for half in (low_half, high_half):
        main_halves.append(half[:, :main_each].reshape(-1, width))
        rest = half[:, main_each:].reshape(-1, width)
        block = rest[:tower_half]
        tower_width = tower.shape[2]
        tower_halves.append(
            jnp.concatenate([block[:, :tower_width], block[:, tower_width:]], 0).reshape(
                tower.shape
            )
        )
        at = tower_half
        gate_halves.append(rest[at : at + gate_block.shape[0]].reshape(gates.shape))
        at += gate_block.shape[0]
        vector_halves.append(
            rest[at : at + vector_rows].reshape(-1)[: vector_flat.shape[0]].reshape(vector.shape)
        )
    return (
        jnp.concatenate(main_halves, 1).astype(F32),
        jnp.concatenate(gate_halves, 0).astype(F32).T,
        jnp.concatenate(tower_halves, 0).astype(F32),
        jnp.concatenate(vector_halves, 0).astype(F32),
    )


def solution(mesh):
    return jax.shard_map(
        on_device,
        mesh=mesh,
        in_specs=(
            P(("grp", "ep"), None),
            P(("grp", "ep"), None),
            P(),
            P("ep", None, "mp"),
            P("ep", "mp", None),
            P(),
            P(),
            P(),
            P(),
            P(("grp", "ep", "mp"), None),
            P(("grp", "ep", "mp"), None),
        ),
        out_specs=(P(), P(), P(), P()),
        check_vma=False,
    )
```

```python
import math

import jax
import jax.numpy as jnp
from jax import lax
from jax.experimental import pallas as pl
from jax.experimental.pallas import tpu as pltpu
from jax.sharding import PartitionSpec as P

F32 = jnp.float32
BF16 = jnp.bfloat16
SLOT_CHUNKS = 2
CHIPS = ("ep", "mp")
GATE_STEPS = 3


def swap(shard, axis):
    return lax.ppermute(shard, axis, [(0, 1), (1, 0)])


def unpack_kernel(group_ref, own_ref, other_ref, main_ref, tower_ref, gate_ref, vector_ref):
    blocks, parts, _, width = own_ref.shape
    main_rows = main_ref.shape[1] // blocks
    tower_rows = tower_ref.shape[2] // blocks
    tower_width = tower_ref.shape[3]
    gate_steps = gate_ref.shape[1] // blocks
    first = group_ref[0] == 0
    step = pl.program_id(0)

    def both(block, part):
        own = own_ref[block, part].astype(F32)
        other = other_ref[block, part].astype(F32)
        return jnp.where(first, own, other), jnp.where(first, other, own)

    for block in range(blocks):
        tower_sum = [0.0, 0.0]
        vector_sum = [0.0, 0.0]
        for part in range(parts):
            for half, value in enumerate(both(block, part)):
                main_ref[
                    part,
                    block * main_rows : (block + 1) * main_rows,
                    half * width : (half + 1) * width,
                ] = value[:main_rows]
                rest = value[main_rows : main_rows + 2]
                tower_sum[half] += value[main_rows + 2 : main_rows + 2 + tower_rows]
                vector_sum[half] += rest

                @pl.when(step < GATE_STEPS)
                def _(rest=rest, part=part, half=half):
                    for row in range(2):
                        at = (part * 2 + row) * width
                        gate_ref[half, block : block + 1, at : at + width] = rest[row : row + 1]

        for half in range(2):
            rows = slice(block * tower_rows, (block + 1) * tower_rows)
            tower_ref[half, 0, rows, :] = tower_sum[half][:, :tower_width]
            tower_ref[half, 1, rows, :] = tower_sum[half][:, tower_width:]
            if block == 0:

                @pl.when(step == GATE_STEPS)
                def _(half=half, vector=vector_sum[half]):
                    vector_ref[half] = vector


def unpack(own_half, other_half, group_index, chips, parts):
    _, each, width = own_half.shape
    outer = chips // parts
    step_blocks = 8
    steps = outer // step_blocks
    main_rows, tower_rows = each - 8, 6
    tower_width = width // 2
    shape = (outer, parts, each, width)
    block = pl.BlockSpec((step_blocks, parts, each, width), lambda i, g: (i, 0, 0, 0))
    return pl.pallas_call(
        unpack_kernel,
        grid_spec=pltpu.PrefetchScalarGridSpec(
            num_scalar_prefetch=1,
            grid=(steps,),
            in_specs=[block, block],
            out_specs=[
                pl.BlockSpec((parts, step_blocks * main_rows, 2 * width), lambda i, g: (0, i, 0)),
                pl.BlockSpec(
                    (2, 2, step_blocks * tower_rows, tower_width), lambda i, g: (0, 0, i, 0)
                ),
                pl.BlockSpec(
                    (2, step_blocks, 2 * parts * width),
                    lambda i, g: (0, jnp.minimum(i, GATE_STEPS - 1), 0),
                ),
                pl.BlockSpec((2, 2, width), lambda i, g: (0, 0, 0)),
            ],
        ),
        out_shape=[
            jax.ShapeDtypeStruct((parts, outer * main_rows, 2 * width), F32),
            jax.ShapeDtypeStruct((2, 2, outer * tower_rows, tower_width), F32),
            jax.ShapeDtypeStruct((2, GATE_STEPS * step_blocks, 2 * parts * width), F32),
            jax.ShapeDtypeStruct((2, 2, width), F32),
        ],
        compiler_params=pltpu.CompilerParams(vmem_limit_bytes=32 * 1024 * 1024),
    )(
        group_index.astype(jnp.int32).reshape(1),
        own_half.reshape(shape),
        other_half.reshape(shape),
    )


def student_grads(rows_in, experts_w, gates_w, tower_w, tower_v, soft_labels, masks, loss_scale):
    count_rows = rows_in.shape[0]
    task_count, expert_width, tower_width = tower_w.shape
    expert_count = gates_w.shape[1] // task_count
    pre_act = jnp.dot(rows_in, experts_w, preferred_element_type=F32)
    activation, gelu_back = jax.vjp(jax.nn.gelu, pre_act)
    act_three = activation.reshape(count_rows, expert_count, expert_width)
    gate_logit = jnp.dot(rows_in, gates_w, preferred_element_type=F32).reshape(
        count_rows, task_count, expert_count
    )
    gate_sig = jax.nn.sigmoid(gate_logit)
    gate_sum = jnp.sum(gate_sig, -1, keepdims=True)
    gate_share = gate_sig / gate_sum
    mixture = jnp.einsum("ntk,nks->nts", gate_share, act_three).astype(BF16)
    tower_pre = jnp.einsum("nts,tsh->nth", mixture, tower_w, preferred_element_type=F32)
    tower_sig = jax.nn.sigmoid(tower_pre)
    tower_hid = tower_pre * tower_sig
    tower_vec = tower_v.astype(F32)
    task_logit = jnp.einsum("nth,th->nt", tower_hid, tower_vec)
    logit_grad = masks * (jax.nn.sigmoid(task_logit) - soft_labels) * loss_scale
    grad_tower_out = jnp.einsum("nt,nth->th", logit_grad, tower_hid)
    hid_grad = logit_grad[:, :, None] * tower_vec[None, :, :]
    tower_grad = (hid_grad * tower_sig * (1.0 + tower_pre * (1.0 - tower_sig))).astype(BF16)
    grad_tower_in = jnp.einsum("nts,nth->tsh", mixture, tower_grad, preferred_element_type=F32)
    mixture_grad = jnp.einsum("nth,tsh->nts", tower_grad, tower_w, preferred_element_type=F32)
    act_grad = jnp.einsum("ntk,nts->nks", gate_share, mixture_grad)
    share_grad = jnp.einsum("nts,nks->ntk", mixture_grad, act_three)
    sig_grad = (share_grad - jnp.sum(gate_share * share_grad, -1, keepdims=True)) / gate_sum
    gate_grad = (
        (sig_grad * gate_sig * (1.0 - gate_sig))
        .astype(BF16)
        .reshape(count_rows, task_count * expert_count)
    )
    pre_grad = gelu_back(act_grad.reshape(count_rows, expert_count * expert_width))[0].astype(BF16)
    return pre_grad, gate_grad, grad_tower_in, grad_tower_out


def on_device(
    teacher_rows,
    expert_ids,
    router,
    teacher_up,
    teacher_down,
    student_experts,
    student_gates,
    tower_in,
    tower_out,
    soft_labels,
    label_masks,
):
    rows_dev, feature_dim = teacher_rows.shape
    expert_total = lax.axis_size("ep")
    width_parts = lax.axis_size("mp")
    group_index = lax.axis_index("grp")
    chips = expert_total * width_parts
    capacity = 4 * rows_dev // expert_total
    chunk_slots = capacity // SLOT_CHUNKS

    labels = swap(jnp.concatenate([soft_labels, label_masks.astype(F32)], 1), "grp")
    task_count = soft_labels.shape[1]

    experts = jnp.arange(expert_total, dtype=jnp.int32)
    hot = [(expert_ids[:, c : c + 1] == experts[None, :]) for c in range(2)]
    named = (hot[0] | hot[1]).astype(BF16)
    sample = jnp.arange(rows_dev, dtype=jnp.int32)
    before = (sample[None, :] < sample[:, None]).astype(BF16)
    earlier = jnp.dot(before, named, preferred_element_type=F32)
    slots = [jnp.sum(jnp.where(h, earlier, 0.0), 1, keepdims=True).astype(jnp.int32) for h in hot]

    def places(chunk):
        found = []
        for c in range(2):
            local = slots[c] - chunk * chunk_slots
            inside = (local >= 0) & (local < chunk_slots)
            found.append(jnp.where(inside, expert_ids[:, c : c + 1] * chunk_slots + local, -1))
        return found

    lane = jnp.arange(expert_total * chunk_slots, dtype=jnp.int32)[None, :]
    targets = [places(chunk) for chunk in range(SLOT_CHUNKS)]

    received = []
    for first, second in targets:
        pick = ((lane == first) | (lane == second)).astype(BF16)
        outgoing = lax.dot_general(
            pick, teacher_rows, (((0,), (0,)), ((), ())), preferred_element_type=F32
        ).astype(BF16)
        outgoing = outgoing.reshape(expert_total, chunk_slots, feature_dim)
        received.append(lax.all_to_all(outgoing, "ep", split_axis=0, concat_axis=0, tiled=True))

    logits = jnp.dot(teacher_rows, router, preferred_element_type=F32)
    chosen = [jnp.sum(jnp.where(h, logits, 0.0), 1, keepdims=True) for h in hot]
    sigs = [jax.nn.sigmoid(v) for v in chosen]
    weights = [v / (sigs[0] + sigs[1]) for v in sigs]

    up_proj = teacher_up[0]
    down_proj = teacher_down[0]
    part = lax.axis_index("mp")
    half_width = feature_dim // width_parts
    mixed = jnp.zeros((rows_dev, half_width), F32)
    wide_lane = jnp.arange(chips * chunk_slots, dtype=jnp.int32)[None, :]
    wide_expert = wide_lane // (width_parts * chunk_slots)
    wide_place = wide_expert * chunk_slots + wide_lane % chunk_slots
    for chunk in range(SLOT_CHUNKS):
        rows_in = received[chunk].reshape(expert_total * chunk_slots, feature_dim)
        inner = jax.nn.gelu(jnp.dot(rows_in, up_proj, preferred_element_type=F32)).astype(BF16)
        partial = jnp.dot(inner, down_proj, preferred_element_type=F32).astype(BF16)
        outgoing = partial.reshape(expert_total, chunk_slots, width_parts, half_width)
        outgoing = outgoing.transpose(0, 2, 1, 3).reshape(chips, chunk_slots, half_width)
        returned = lax.all_to_all(outgoing, CHIPS, split_axis=0, concat_axis=0, tiled=True)
        returned = returned.reshape(chips * chunk_slots, half_width)
        first, second = targets[chunk]
        share = jnp.where(wide_place == first, weights[0], 0.0) + jnp.where(
            wide_place == second, weights[1], 0.0
        )
        high = share.astype(BF16)
        low = (share - high.astype(F32)).astype(BF16)
        mixed = mixed + jnp.dot(high, returned, preferred_element_type=F32)
        mixed = mixed + jnp.dot(low, returned, preferred_element_type=F32)
    mixed = mixed.astype(BF16)

    half_rows = rows_dev // width_parts
    kept = lax.dynamic_slice_in_dim(mixed, part * half_rows, half_rows, 0)
    given = lax.dynamic_slice_in_dim(mixed, (1 - part) * half_rows, half_rows, 0)
    taken = swap(given, "mp")
    own_rows = jnp.concatenate(
        [jnp.where(part == 0, kept, taken), jnp.where(part == 0, taken, kept)], 1
    )
    kept_both = jnp.concatenate([kept, given], 0)
    all_rows = jnp.concatenate([kept_both, swap(kept_both, "grp")], 0)

    sample_total = rows_dev * lax.axis_size("grp") * expert_total
    pre_grad, gate_grad, grad_tower_in, grad_tower_out = student_grads(
        own_rows,
        student_experts,
        student_gates,
        tower_in,
        tower_out,
        labels[:, :task_count],
        labels[:, task_count:],
        1.0 / math.sqrt(sample_total),
    )

    def halves(array, axis):
        size = array.shape[axis] // 2
        mine = lax.dynamic_slice_in_dim(array, group_index * size, size, axis)
        theirs = lax.dynamic_slice_in_dim(array, (1 - group_index) * size, size, axis)
        return mine, theirs

    mine, theirs = halves(pre_grad, 1)
    gate_mine, gate_theirs = halves(gate_grad, 1)
    width, gate_width = mine.shape[1], gate_mine.shape[1]
    mine = jnp.concatenate([mine, gate_mine], 1)
    theirs = swap(jnp.concatenate([theirs, gate_theirs], 1), "grp")
    from_other = swap(jnp.concatenate([mine, theirs], 0), "mp")
    factors = jnp.concatenate([mine, from_other[:half_rows], theirs, from_other[half_rows:]], 0)
    contract = (((0,), (0,)), ((), ()))
    main = lax.dot_general(all_rows, factors[:, :width], contract, preferred_element_type=F32)
    gates = lax.dot_general(factors[:, width:], all_rows, contract, preferred_element_type=F32)
    mine, theirs = halves(grad_tower_in.astype(BF16), 0)
    tower = (mine.astype(F32) + swap(theirs, "grp").astype(F32)).reshape(-1, grad_tower_in.shape[2])
    mine, theirs = halves(grad_tower_out.astype(BF16), 0)
    vector = (mine.astype(F32) + swap(theirs, "grp").astype(F32)).reshape(-1)

    tower_half = tower.shape[0] // 2
    tower = jnp.concatenate([tower[:tower_half], tower[tower_half:]], 1)
    rest = jnp.concatenate(
        [
            gates.reshape(-1),
            vector,
            jnp.zeros((2 * expert_total * width - gates.size - vector.size,), F32),
        ]
    )
    packed = jnp.concatenate(
        [
            main.astype(BF16).reshape(expert_total, -1, width),
            rest.astype(BF16).reshape(expert_total, -1, width),
            tower.astype(BF16).reshape(expert_total, -1, width),
        ],
        1,
    )

    parts = lax.all_to_all(packed, "ep", split_axis=0, concat_axis=0, tiled=True)
    total = jnp.sum(parts.astype(F32), 0).astype(BF16)
    spread = jnp.broadcast_to(total[None], (chips,) + total.shape)
    own_half = lax.all_to_all(spread, CHIPS, split_axis=0, concat_axis=0, tiled=True)
    other_half = swap(own_half, "grp")
    main, tower, gates, vector = unpack(own_half, other_half, group_index, chips, width_parts)
    return (
        main.reshape(student_experts.shape),
        gates.reshape(2 * gate_width, feature_dim).T,
        tower.reshape(tower_in.shape),
        vector.reshape(2, -1)[:, : tower_out.size // 2].reshape(tower_out.shape),
    )


def solution(mesh):
    return jax.shard_map(
        on_device,
        mesh=mesh,
        in_specs=(
            P(("grp", "ep"), None),
            P(("grp", "ep"), None),
            P(),
            P("ep", None, "mp"),
            P("ep", "mp", None),
            P(),
            P(),
            P(),
            P(),
            P(("grp", "ep", "mp"), None),
            P(("grp", "ep", "mp"), None),
        ),
        out_specs=(P(), P(), P(), P()),
        check_vma=False,
    )
```

```python
import functools
import math

import jax
import jax.numpy as jnp
from jax import lax
from jax.experimental import pallas as pl
from jax.experimental.pallas import tpu as pltpu
from jax.sharding import PartitionSpec as P

F32 = jnp.float32
BF16 = jnp.bfloat16
SLOT_CHUNKS = 2
CHIPS = ("ep", "mp")
GATE_STEPS = 3


def swap(shard, axis):
    return lax.ppermute(shard, axis, [(0, 1), (1, 0)])


def unpack_kernel(place_ref, half_ref, *refs):
    main_ref, tower_ref, gate_ref, vector_ref = refs[-4:]
    blocks, parts, _, width = half_ref.shape
    main_rows = main_ref.shape[1] // blocks
    tower_rows = tower_ref.shape[2] // blocks
    tower_width = tower_ref.shape[3]
    step = pl.program_id(0)
    for block in range(blocks):
        values = [half_ref[block, part].astype(F32) for part in range(parts)]
        for part in range(parts):
            main_ref[part, block * main_rows : (block + 1) * main_rows, :] = values[part][
                :main_rows
            ]
        tower = sum(value[main_rows + 2 : main_rows + 2 + tower_rows] for value in values)
        rows = slice(block * tower_rows, (block + 1) * tower_rows)
        tower_ref[0, 0, rows, :] = tower[:, :tower_width]
        tower_ref[0, 1, rows, :] = tower[:, tower_width:]
        rests = [value[main_rows : main_rows + 2] for value in values]

        @pl.when(step < GATE_STEPS)
        def _(rests=rests, block=block):
            for part in range(parts):
                for row in range(2):
                    at = (part * 2 + row) * width
                    gate_ref[0, block : block + 1, at : at + width] = rests[part][row : row + 1]

        if block == 0:

            @pl.when(step == GATE_STEPS)
            def _(rests=rests):
                vector_ref[0] = sum(rests)


def unpack(half, place, chips, parts, filled):
    _, each, width = half.shape
    outer = chips // parts
    step_blocks = 8
    main_rows, tower_rows = each - 8, 6
    tower_width = width // 2
    out_shape = [
        jax.ShapeDtypeStruct((parts, outer * main_rows, 2 * width), F32),
        jax.ShapeDtypeStruct((2, 2, outer * tower_rows, tower_width), F32),
        jax.ShapeDtypeStruct((2, GATE_STEPS * step_blocks, 2 * parts * width), F32),
        jax.ShapeDtypeStruct((2, 2, width), F32),
    ]
    size = sum(4 * math.prod(shape.shape) for shape in out_shape) // 2 + 2 * half.size
    return pl.pallas_call(
        unpack_kernel,
        grid_spec=pltpu.PrefetchScalarGridSpec(
            num_scalar_prefetch=1,
            grid=(outer // step_blocks,),
            in_specs=[pl.BlockSpec((step_blocks, parts, each, width), lambda i, g: (i, 0, 0, 0))]
            + [pl.BlockSpec(memory_space=pl.ANY)] * len(filled),
            out_specs=[
                pl.BlockSpec((parts, step_blocks * main_rows, width), lambda i, g: (0, i, g[0])),
                pl.BlockSpec(
                    (1, 2, step_blocks * tower_rows, tower_width), lambda i, g: (g[0], 0, i, 0)
                ),
                pl.BlockSpec(
                    (1, step_blocks, 2 * parts * width),
                    lambda i, g: (g[0], jnp.minimum(i, GATE_STEPS - 1), 0),
                ),
                pl.BlockSpec((1, 2, width), lambda i, g: (g[0], 0, 0)),
            ],
        ),
        out_shape=out_shape,
        input_output_aliases={2 + i: i for i in range(len(filled))},
        cost_estimate=pl.CostEstimate(flops=half.size, bytes_accessed=size, transcendentals=0),
        compiler_params=pltpu.CompilerParams(vmem_limit_bytes=32 * 1024 * 1024),
    )(place.astype(jnp.int32).reshape(1), half.reshape(outer, parts, each, width), *filled)


def student_kernel(
    part_ref,
    kept_ref,
    taken_ref,
    experts_ref,
    gates_ref,
    tower_in_ref,
    tower_out_ref,
    labels_ref,
    pre_grad_ref,
    gate_grad_ref,
    tower_in_grad_ref,
    tower_out_grad_ref,
    act_ref,
    slope_ref,
    *,
    loss_scale,
):
    tasks, width, _ = tower_in_ref.shape
    columns = gates_ref.shape[0]
    experts = columns // tasks
    half = kept_ref.shape[1]
    first = part_ref[0] == 0
    left = jnp.where(first, kept_ref[...], taken_ref[...])
    right = jnp.where(first, taken_ref[...], kept_ref[...])
    across = (((1,), (1,)), ((), ()))
    down = (((0,), (0,)), ((), ()))

    logit = lax.dot_general(left, gates_ref[:, :half], across, preferred_element_type=F32)
    logit += lax.dot_general(right, gates_ref[:, half:], across, preferred_element_type=F32)
    sig = jax.nn.sigmoid(logit)
    task_of = [lax.broadcasted_iota(jnp.int32, (columns, columns), d) // experts for d in (0, 1)]
    same_task = jnp.where(task_of[0] == task_of[1], 1.0, 0.0)

    def task_sum(value):
        return jnp.dot(
            value, same_task, precision=lax.Precision.HIGHEST, preferred_element_type=F32
        )

    gate_sum = task_sum(sig)
    share = sig / gate_sum

    scale = math.sqrt(2.0 / math.pi)
    for k in range(experts):
        at = slice(k * width, (k + 1) * width)
        pre = jnp.dot(left, experts_ref[:half, at], preferred_element_type=F32)
        pre += jnp.dot(right, experts_ref[half:, at], preferred_element_type=F32)
        square = pre * pre
        tanh = jnp.tanh(scale * (pre + 0.044715 * (square * pre)))
        cdf = 0.5 * (1.0 + tanh)
        act_ref[k] = pre * cdf
        slope_ref[k] = cdf + (0.5 * scale) * pre * (1.0 - tanh * tanh) * (
            1.0 + (3 * 0.044715) * square
        )

    mix_grads = []
    lane = lax.broadcasted_iota(jnp.int32, share.shape, 1)
    share_grad = jnp.zeros(share.shape, F32)
    for t in range(tasks):
        mixture = jnp.zeros(act_ref.shape[1:], F32)
        for k in range(experts):
            column = t * experts + k
            mixture += share[:, column : column + 1] * act_ref[k]
        mixture = mixture.astype(BF16)
        tower_w = tower_in_ref[t]
        tower_pre = jnp.dot(mixture, tower_w, preferred_element_type=F32)
        tower_sig = jax.nn.sigmoid(tower_pre)
        tower_hid = tower_pre * tower_sig
        tower_vec = tower_out_ref[t : t + 1, :].astype(F32)
        task_logit = jnp.sum(tower_hid * tower_vec, 1, keepdims=True)
        mask = labels_ref[:, tasks + t : tasks + t + 1]
        error = jax.nn.sigmoid(task_logit) - labels_ref[:, t : t + 1]
        logit_grad = mask * error * loss_scale
        tower_out_grad_ref[t : t + 1, :] = jnp.sum(logit_grad * tower_hid, 0, keepdims=True)
        tower_grad = (
            (logit_grad * tower_vec) * tower_sig * (1.0 + tower_pre * (1.0 - tower_sig))
        ).astype(BF16)
        tower_in_grad_ref[t] = lax.dot_general(
            mixture, tower_grad, down, preferred_element_type=F32
        ).astype(BF16)
        mix_grad = lax.dot_general(tower_grad, tower_w, across, preferred_element_type=F32)
        mix_grads.append(mix_grad)
        for k in range(experts):
            value = jnp.sum(mix_grad * act_ref[k], 1, keepdims=True)
            share_grad = jnp.where(lane == t * experts + k, value, share_grad)

    for k in range(experts):
        act_grad = jnp.zeros(act_ref.shape[1:], F32)
        for t in range(tasks):
            column = t * experts + k
            act_grad += share[:, column : column + 1] * mix_grads[t]
        pre_grad_ref[:, k * width : (k + 1) * width] = (act_grad * slope_ref[k]).astype(BF16)

    sig_grad = (share_grad - task_sum(share * share_grad)) / gate_sum
    gate_grad_ref[...] = (sig_grad * sig * (1.0 - sig)).astype(BF16)


def student_grads(part, kept, taken, experts_w, gates_w, tower_w, tower_v, labels, loss_scale):
    rows = kept.shape[0]
    width = tower_w.shape[1]
    experts = experts_w.shape[1] // width
    vmem = pl.BlockSpec(memory_space=pltpu.VMEM)
    return pl.pallas_call(
        functools.partial(student_kernel, loss_scale=loss_scale),
        in_specs=[pl.BlockSpec(memory_space=pltpu.SMEM)] + [vmem] * 7,
        out_specs=[vmem] * 4,
        out_shape=[
            jax.ShapeDtypeStruct((rows, experts_w.shape[1]), BF16),
            jax.ShapeDtypeStruct((rows, gates_w.shape[1]), BF16),
            jax.ShapeDtypeStruct(tower_w.shape, BF16),
            jax.ShapeDtypeStruct(tower_v.shape, F32),
        ],
        scratch_shapes=[pltpu.VMEM((experts, rows, width), F32)] * 2,
        cost_estimate=pl.CostEstimate(
            flops=2 * rows * experts_w.size, bytes_accessed=2 * experts_w.size, transcendentals=0
        ),
        compiler_params=pltpu.CompilerParams(vmem_limit_bytes=32 * 1024 * 1024),
    )(part.reshape(1), kept, taken, experts_w, gates_w.T, tower_w, tower_v, labels)


def on_device(
    teacher_rows,
    expert_ids,
    router,
    teacher_up,
    teacher_down,
    student_experts,
    student_gates,
    tower_in,
    tower_out,
    soft_labels,
    label_masks,
):
    rows_dev, feature_dim = teacher_rows.shape
    expert_total = lax.axis_size("ep")
    width_parts = lax.axis_size("mp")
    group_index = lax.axis_index("grp")
    chips = expert_total * width_parts
    capacity = 4 * rows_dev // expert_total
    chunk_slots = capacity // SLOT_CHUNKS

    labels = swap(jnp.concatenate([soft_labels, label_masks.astype(F32)], 1), "grp")

    experts = jnp.arange(expert_total, dtype=jnp.int32)
    hot = [(expert_ids[:, c : c + 1] == experts[None, :]) for c in range(2)]
    named = (hot[0] | hot[1]).astype(BF16)
    sample = jnp.arange(rows_dev, dtype=jnp.int32)
    before = (sample[None, :] < sample[:, None]).astype(BF16)
    earlier = jnp.dot(before, named, preferred_element_type=F32)
    slots = [jnp.sum(jnp.where(h, earlier, 0.0), 1, keepdims=True).astype(jnp.int32) for h in hot]

    def places(chunk):
        found = []
        for c in range(2):
            local = slots[c] - chunk * chunk_slots
            inside = (local >= 0) & (local < chunk_slots)
            found.append(jnp.where(inside, expert_ids[:, c : c + 1] * chunk_slots + local, -1))
        return found

    lane = jnp.arange(expert_total * chunk_slots, dtype=jnp.int32)[None, :]
    targets = [places(chunk) for chunk in range(SLOT_CHUNKS)]

    received = []
    for first, second in targets:
        pick = ((lane == first) | (lane == second)).astype(BF16)
        outgoing = lax.dot_general(
            pick, teacher_rows, (((0,), (0,)), ((), ())), preferred_element_type=F32
        ).astype(BF16)
        outgoing = outgoing.reshape(expert_total, chunk_slots, feature_dim)
        received.append(lax.all_to_all(outgoing, "ep", split_axis=0, concat_axis=0, tiled=True))

    logits = jnp.dot(teacher_rows, router, preferred_element_type=F32)
    chosen = [jnp.sum(jnp.where(h, logits, 0.0), 1, keepdims=True) for h in hot]
    sigs = [jax.nn.sigmoid(v) for v in chosen]
    weights = [v / (sigs[0] + sigs[1]) for v in sigs]

    up_proj = teacher_up[0]
    down_proj = teacher_down[0]
    part = lax.axis_index("mp")
    half_width = feature_dim // width_parts
    mixed = jnp.zeros((rows_dev, half_width), F32)
    wide_lane = jnp.arange(chips * chunk_slots, dtype=jnp.int32)[None, :]
    wide_expert = wide_lane // (width_parts * chunk_slots)
    wide_place = wide_expert * chunk_slots + wide_lane % chunk_slots
    for chunk in range(SLOT_CHUNKS):
        rows_in = received[chunk].reshape(expert_total * chunk_slots, feature_dim)
        inner = jax.nn.gelu(jnp.dot(rows_in, up_proj, preferred_element_type=F32)).astype(BF16)
        partial = jnp.dot(inner, down_proj, preferred_element_type=F32).astype(BF16)
        outgoing = partial.reshape(expert_total, chunk_slots, width_parts, half_width)
        outgoing = outgoing.transpose(0, 2, 1, 3).reshape(chips, chunk_slots, half_width)
        returned = lax.all_to_all(outgoing, CHIPS, split_axis=0, concat_axis=0, tiled=True)
        returned = returned.reshape(chips * chunk_slots, half_width)
        first, second = targets[chunk]
        share = jnp.where(wide_place == first, weights[0], 0.0) + jnp.where(
            wide_place == second, weights[1], 0.0
        )
        high = share.astype(BF16)
        low = (share - high.astype(F32)).astype(BF16)
        mixed = mixed + jnp.dot(high, returned, preferred_element_type=F32)
        mixed = mixed + jnp.dot(low, returned, preferred_element_type=F32)
    mixed = mixed.astype(BF16)

    half_rows = rows_dev // width_parts
    kept = lax.dynamic_slice_in_dim(mixed, part * half_rows, half_rows, 0)
    given = lax.dynamic_slice_in_dim(mixed, (1 - part) * half_rows, half_rows, 0)
    taken = swap(given, "mp")
    kept_both = jnp.concatenate([kept, given], 0)
    all_rows = jnp.concatenate([kept_both, swap(kept_both, "grp")], 0)

    sample_total = rows_dev * lax.axis_size("grp") * expert_total
    pre_grad, gate_grad, grad_tower_in, grad_tower_out = student_grads(
        part,
        kept,
        taken,
        student_experts,
        student_gates,
        tower_in,
        tower_out,
        labels,
        1.0 / math.sqrt(sample_total),
    )

    def halves(array, axis):
        size = array.shape[axis] // 2
        mine = lax.dynamic_slice_in_dim(array, group_index * size, size, axis)
        theirs = lax.dynamic_slice_in_dim(array, (1 - group_index) * size, size, axis)
        return mine, theirs

    mine, theirs = halves(pre_grad, 1)
    gate_mine, gate_theirs = halves(gate_grad, 1)
    width, gate_width = mine.shape[1], gate_mine.shape[1]
    mine = jnp.concatenate([mine, gate_mine], 1)
    theirs = swap(jnp.concatenate([theirs, gate_theirs], 1), "grp")
    from_other = swap(jnp.concatenate([mine, theirs], 0), "mp")
    factors = jnp.concatenate([mine, from_other[:half_rows], theirs, from_other[half_rows:]], 0)
    contract = (((0,), (0,)), ((), ()))
    main = lax.dot_general(all_rows, factors[:, :width], contract, preferred_element_type=F32)
    gates = lax.dot_general(factors[:, width:], all_rows, contract, preferred_element_type=F32)
    mine, theirs = halves(grad_tower_in, 0)
    tower = (mine.astype(F32) + swap(theirs, "grp").astype(F32)).reshape(-1, grad_tower_in.shape[2])
    mine, theirs = halves(grad_tower_out.astype(BF16), 0)
    vector = (mine.astype(F32) + swap(theirs, "grp").astype(F32)).reshape(-1)

    tower_half = tower.shape[0] // 2
    tower = jnp.concatenate([tower[:tower_half], tower[tower_half:]], 1)
    rest = jnp.concatenate(
        [
            gates.reshape(-1),
            vector,
            jnp.zeros((2 * expert_total * width - gates.size - vector.size,), F32),
        ]
    )
    packed = jnp.concatenate(
        [
            main.astype(BF16).reshape(expert_total, -1, width),
            rest.astype(BF16).reshape(expert_total, -1, width),
            tower.astype(BF16).reshape(expert_total, -1, width),
        ],
        1,
    )

    parts = lax.all_to_all(packed, "ep", split_axis=0, concat_axis=0, tiled=True)
    total = jnp.sum(parts.astype(F32), 0).astype(BF16)
    spread = jnp.broadcast_to(total[None], (chips,) + total.shape)
    own_half = lax.all_to_all(spread, CHIPS, split_axis=0, concat_axis=0, tiled=True)
    other_half = swap(own_half, "grp")
    filled = unpack(own_half, group_index, chips, width_parts, ())
    main, tower, gates, vector = unpack(other_half, 1 - group_index, chips, width_parts, filled)
    return (
        main.reshape(student_experts.shape),
        gates.reshape(2 * gate_width, feature_dim).T,
        tower.reshape(tower_in.shape),
        vector.reshape(2, -1)[:, : tower_out.size // 2].reshape(tower_out.shape),
    )


def solution(mesh):
    return jax.shard_map(
        on_device,
        mesh=mesh,
        in_specs=(
            P(("grp", "ep"), None),
            P(("grp", "ep"), None),
            P(),
            P("ep", None, "mp"),
            P("ep", "mp", None),
            P(),
            P(),
            P(),
            P(),
            P(("grp", "ep", "mp"), None),
            P(("grp", "ep", "mp"), None),
        ),
        out_specs=(P(), P(), P(), P()),
        check_vma=False,
    )
```

```python
import functools
import math

import jax
import jax.numpy as jnp
from jax import lax
from jax.experimental import pallas as pl
from jax.experimental.pallas import tpu as pltpu
from jax.sharding import PartitionSpec as P

F32 = jnp.float32
BF16 = jnp.bfloat16
SLOT_CHUNKS = 2
CHIPS = ("ep", "mp")
PIECE = 2
GATE_STEPS = 3


def swap(shard, axis):
    return lax.ppermute(shard, axis, [(0, 1), (1, 0)])


def unpack_kernel(place_ref, half_ref, *refs):
    main_ref, tower_ref, gate_ref, vector_ref = refs[-4:]
    blocks, parts, _, width = half_ref.shape
    main_rows = main_ref.shape[1] // blocks
    tower_rows = tower_ref.shape[2] // blocks
    tower_width = tower_ref.shape[3]
    step = pl.program_id(0)
    for block in range(blocks):
        values = [half_ref[block, part].astype(F32) for part in range(parts)]
        for part in range(parts):
            main_ref[part, block * main_rows : (block + 1) * main_rows, :] = values[part][
                :main_rows
            ]
        tower = sum(value[main_rows + 2 : main_rows + 2 + tower_rows] for value in values)
        rows = slice(block * tower_rows, (block + 1) * tower_rows)
        tower_ref[0, 0, rows, :] = tower[:, :tower_width]
        tower_ref[0, 1, rows, :] = tower[:, tower_width:]
        rests = [value[main_rows : main_rows + 2] for value in values]

        @pl.when(step < GATE_STEPS)
        def _(rests=rests, block=block):
            for part in range(parts):
                for row in range(2):
                    at = (part * 2 + row) * width
                    gate_ref[0, block : block + 1, at : at + width] = rests[part][row : row + 1]

        if block == 0:

            @pl.when(step == GATE_STEPS)
            def _(rests=rests):
                vector_ref[0] = sum(rests)


def unpack(half, place, chips, parts, filled):
    _, each, width = half.shape
    outer = chips // parts
    step_blocks = 8
    main_rows, tower_rows = each - 8, 6
    tower_width = width // 2
    out_shape = [
        jax.ShapeDtypeStruct((parts, outer * main_rows, 2 * width), F32),
        jax.ShapeDtypeStruct((2, 2, outer * tower_rows, tower_width), F32),
        jax.ShapeDtypeStruct((2, GATE_STEPS * step_blocks, 2 * parts * width), F32),
        jax.ShapeDtypeStruct((2, 2, width), F32),
    ]
    size = sum(4 * math.prod(shape.shape) for shape in out_shape) // 2 + 2 * half.size
    return pl.pallas_call(
        unpack_kernel,
        grid_spec=pltpu.PrefetchScalarGridSpec(
            num_scalar_prefetch=1,
            grid=(outer // step_blocks,),
            in_specs=[pl.BlockSpec((step_blocks, parts, each, width), lambda i, g: (i, 0, 0, 0))]
            + [pl.BlockSpec(memory_space=pl.ANY)] * len(filled),
            out_specs=[
                pl.BlockSpec((parts, step_blocks * main_rows, width), lambda i, g: (0, i, g[0])),
                pl.BlockSpec(
                    (1, 2, step_blocks * tower_rows, tower_width), lambda i, g: (g[0], 0, i, 0)
                ),
                pl.BlockSpec(
                    (1, step_blocks, 2 * parts * width),
                    lambda i, g: (g[0], jnp.minimum(i, GATE_STEPS - 1), 0),
                ),
                pl.BlockSpec((1, 2, width), lambda i, g: (g[0], 0, 0)),
            ],
        ),
        out_shape=out_shape,
        input_output_aliases={2 + i: i for i in range(len(filled))},
        cost_estimate=pl.CostEstimate(flops=half.size, bytes_accessed=size, transcendentals=0),
        compiler_params=pltpu.CompilerParams(vmem_limit_bytes=32 * 1024 * 1024),
    )(place.astype(jnp.int32).reshape(1), half.reshape(outer, parts, each, width), *filled)


def dispatch_kernel(ids_ref, rows_ref, out_ref, target_ref, *, experts, first_slot):
    step = pl.program_id(0)
    count = rows_ref.shape[0]
    block_experts, slots, _ = out_ref.shape

    @pl.when(step == 0)
    def _():
        ids = ids_ref[...]
        expert = lax.broadcasted_iota(jnp.int32, (experts, count), 0)
        hot = [expert == ids[c : c + 1] for c in range(2)]
        named = jnp.where(hot[0] | hot[1], 1.0, 0.0).astype(BF16)
        order = [lax.broadcasted_iota(jnp.int32, (count, count), d) for d in (0, 1)]
        before = jnp.where(order[0] < order[1], 1.0, 0.0).astype(BF16)
        earlier = jnp.dot(named, before, preferred_element_type=F32)
        for c in range(2):
            slot = jnp.sum(jnp.where(hot[c], earlier, 0.0), 0, keepdims=True).astype(jnp.int32)
            local = slot - first_slot
            inside = (local >= 0) & (local < slots)
            target_ref[c : c + 1, :] = jnp.where(inside, ids[c : c + 1] * slots + local, -1)

    block = block_experts * slots
    place = step * block + lax.broadcasted_iota(jnp.int32, (block, count), 0)
    chosen = (place == target_ref[0:1, :]) | (place == target_ref[1:2, :])
    pick = jnp.where(chosen, 1.0, 0.0).astype(BF16)
    rows = jnp.dot(pick, rows_ref[...], preferred_element_type=F32).astype(BF16)
    out_ref[...] = rows.reshape(out_ref.shape)


def dispatch(ids_by_choice, rows, experts, slots, first_slot):
    count, feature_dim = rows.shape
    block_experts = experts // 2
    return pl.pallas_call(
        functools.partial(dispatch_kernel, experts=experts, first_slot=first_slot),
        grid=(2,),
        in_specs=[
            pl.BlockSpec((2, count), lambda i: (0, 0)),
            pl.BlockSpec((count, feature_dim), lambda i: (0, 0)),
        ],
        out_specs=pl.BlockSpec((block_experts, slots, feature_dim), lambda i: (i, 0, 0)),
        out_shape=jax.ShapeDtypeStruct((experts, slots, feature_dim), BF16),
        scratch_shapes=[pltpu.VMEM((2, count), jnp.int32)],
        cost_estimate=pl.CostEstimate(
            flops=2 * experts * slots * rows.size,
            bytes_accessed=2 * rows.size + 2 * experts * slots * feature_dim,
            transcendentals=0,
        ),
        compiler_params=pltpu.CompilerParams(vmem_limit_bytes=48 * 1024 * 1024),
    )(ids_by_choice, rows)


def combine_kernel(part_ref, high_ref, low_ref, back_ref, so_far_ref, kept_ref, given_ref, both_ref):
    back = back_ref[...]
    mixed = so_far_ref[...] + jnp.dot(high_ref[...], back, preferred_element_type=F32)
    mixed += jnp.dot(low_ref[...], back, preferred_element_type=F32)
    half = kept_ref.shape[0]
    first = part_ref[0] == 0
    top, bottom = mixed[:half], mixed[half:]
    kept = jnp.where(first, top, bottom).astype(BF16)
    given = jnp.where(first, bottom, top).astype(BF16)
    kept_ref[...] = kept
    given_ref[...] = given
    both_ref[:half] = kept
    both_ref[half:] = given


def combine(part, high, low, back, so_far):
    rows, width = so_far.shape
    slots = back.shape[0]
    block = width // 2
    whole = pl.BlockSpec((rows, slots), lambda i: (0, 0))
    half = pl.BlockSpec((rows // 2, block), lambda i: (0, i))
    return pl.pallas_call(
        combine_kernel,
        grid=(width // block,),
        in_specs=[
            pl.BlockSpec(memory_space=pltpu.SMEM),
            whole,
            whole,
            pl.BlockSpec((slots, block), lambda i: (0, i)),
            pl.BlockSpec((rows, block), lambda i: (0, i)),
        ],
        out_specs=[half, half, pl.BlockSpec((rows, block), lambda i: (0, i))],
        out_shape=[
            jax.ShapeDtypeStruct((rows // 2, width), BF16),
            jax.ShapeDtypeStruct((rows // 2, width), BF16),
            jax.ShapeDtypeStruct((rows, width), BF16),
        ],
        cost_estimate=pl.CostEstimate(
            flops=4 * rows * back.size, bytes_accessed=2 * back.size, transcendentals=0
        ),
        compiler_params=pltpu.CompilerParams(vmem_limit_bytes=24 * 1024 * 1024),
    )(part.reshape(1), high, low, back, so_far)


def student_kernel(
    place_ref,
    kept_ref,
    taken_ref,
    experts_ref,
    gates_ref,
    tower_in_ref,
    tower_out_ref,
    labels_ref,
    mine_ref,
    theirs_ref,
    tower_mine_ref,
    tower_theirs_ref,
    act_ref,
    slope_ref,
    *,
    loss_scale,
):
    tasks, width, tower_width = tower_in_ref.shape
    columns = gates_ref.shape[0]
    experts = columns // tasks
    half = kept_ref.shape[1]
    first = place_ref[0] == 0
    group = place_ref[1]
    left = jnp.where(first, kept_ref[...], taken_ref[...])
    right = jnp.where(first, taken_ref[...], kept_ref[...])
    across = (((1,), (1,)), ((), ()))
    down = (((0,), (0,)), ((), ()))

    logit = lax.dot_general(left, gates_ref[:, :half], across, preferred_element_type=F32)
    logit += lax.dot_general(right, gates_ref[:, half:], across, preferred_element_type=F32)
    sig = jax.nn.sigmoid(logit)
    task_of = [lax.broadcasted_iota(jnp.int32, (columns, columns), d) // experts for d in (0, 1)]
    same_task = jnp.where(task_of[0] == task_of[1], 1.0, 0.0)

    def task_sum(value):
        return jnp.dot(
            value, same_task, precision=lax.Precision.HIGHEST, preferred_element_type=F32
        )

    gate_sum = task_sum(sig)
    share = sig / gate_sum

    scale = math.sqrt(2.0 / math.pi)
    per_piece = PIECE
    for k in range(experts):
        if k % per_piece == 0:
            at = slice(k * width, (k + per_piece) * width)
            wide = jnp.dot(left, experts_ref[:half, at], preferred_element_type=F32)
            wide += jnp.dot(right, experts_ref[half:, at], preferred_element_type=F32)
        pre = wide[:, k % per_piece * width : (k % per_piece + 1) * width]
        square = pre * pre
        tanh = jnp.tanh(scale * (pre + 0.044715 * (square * pre)))
        cdf = 0.5 * (1.0 + tanh)
        act_ref[k] = pre * cdf
        slope_ref[k] = cdf + (0.5 * scale) * pre * (1.0 - tanh * tanh) * (
            1.0 + (3 * 0.044715) * square
        )

    mix_grads, tower_in_grads = [], []
    lane = lax.broadcasted_iota(jnp.int32, share.shape, 1)
    share_grad = jnp.zeros(share.shape, F32)
    per_group = tasks // 2
    vector_rows = tower_mine_ref.shape[0] - per_group * width
    vector_row = lax.broadcasted_iota(jnp.int32, (vector_rows, tower_width), 0)
    vectors = [jnp.zeros((vector_rows, tower_width), F32)] * 2
    for t in range(tasks):
        mixture = jnp.zeros(act_ref.shape[1:], F32)
        for k in range(experts):
            column = t * experts + k
            mixture += share[:, column : column + 1] * act_ref[k]
        mixture = mixture.astype(BF16)
        tower_w = tower_in_ref[t]
        tower_pre = jnp.dot(mixture, tower_w, preferred_element_type=F32)
        tower_sig = jax.nn.sigmoid(tower_pre)
        tower_hid = tower_pre * tower_sig
        tower_vec = tower_out_ref[t : t + 1, :].astype(F32)
        task_logit = jnp.sum(tower_hid * tower_vec, 1, keepdims=True)
        mask = labels_ref[:, tasks + t : tasks + t + 1]
        error = jax.nn.sigmoid(task_logit) - labels_ref[:, t : t + 1]
        logit_grad = mask * error * loss_scale
        owner, local = t // per_group, t % per_group
        vectors[owner] = jnp.where(
            vector_row == local,
            jnp.sum(logit_grad * tower_hid, 0, keepdims=True),
            vectors[owner],
        )
        tower_grad = (
            (logit_grad * tower_vec) * tower_sig * (1.0 + tower_pre * (1.0 - tower_sig))
        ).astype(BF16)
        tower_in_grads.append(
            lax.dot_general(mixture, tower_grad, down, preferred_element_type=F32)
        )
        mix_grad = lax.dot_general(tower_grad, tower_w, across, preferred_element_type=F32)
        mix_grads.append(mix_grad)
        for k in range(experts):
            value = jnp.sum(mix_grad * act_ref[k], 1, keepdims=True)
            share_grad = jnp.where(lane == t * experts + k, value, share_grad)

    low_group = group == 0
    for local in range(per_group):
        at = slice(local * width, (local + 1) * width)
        low, high = tower_in_grads[local], tower_in_grads[local + per_group]
        tower_mine_ref[at] = jnp.where(low_group, low, high).astype(BF16)
        tower_theirs_ref[at] = jnp.where(low_group, high, low).astype(BF16)
    tower_mine_ref[per_group * width :] = jnp.where(low_group, vectors[0], vectors[1]).astype(BF16)
    tower_theirs_ref[per_group * width :] = jnp.where(low_group, vectors[1], vectors[0]).astype(
        BF16
    )

    def pre_grad(k):
        act_grad = jnp.zeros(act_ref.shape[1:], F32)
        for t in range(tasks):
            column = t * experts + k
            act_grad += share[:, column : column + 1] * mix_grads[t]
        return act_grad * slope_ref[k]

    for k in range(experts // 2):
        at = slice(k * width, (k + 1) * width)
        low, high = pre_grad(k), pre_grad(k + experts // 2)
        mine_ref[:, at] = jnp.where(low_group, low, high).astype(BF16)
        theirs_ref[:, at] = jnp.where(low_group, high, low).astype(BF16)

    sig_grad = (share_grad - task_sum(share * share_grad)) / gate_sum
    gate_grad = (sig_grad * sig * (1.0 - sig)).astype(BF16)
    end = experts // 2 * width
    lanes = mine_ref.shape[1] - end
    source = lax.broadcasted_iota(jnp.int32, (columns, lanes), 0)
    lane_at = lax.broadcasted_iota(jnp.int32, (columns, lanes), 1)
    for ref, owner in ((mine_ref, group), (theirs_ref, 1 - group)):
        wanted = (source == lane_at + owner * (columns // 2)) & (lane_at < columns // 2)
        move = jnp.where(wanted, 1.0, 0.0).astype(BF16)
        ref[:, end:] = jnp.dot(gate_grad, move, preferred_element_type=F32).astype(BF16)


def student_grads(part, group, kept, taken, experts_w, gates_w, tower_w, tower_v, labels, loss_scale):
    rows = kept.shape[0]
    tasks, width, tower_width = tower_w.shape
    experts = experts_w.shape[1] // width
    vmem = pl.BlockSpec(memory_space=pltpu.VMEM)
    factor = jax.ShapeDtypeStruct((rows, experts_w.shape[1] // 2 + 128), BF16)
    tower = jax.ShapeDtypeStruct((tasks // 2 * width + 16, tower_width), BF16)
    return pl.pallas_call(
        functools.partial(student_kernel, loss_scale=loss_scale),
        in_specs=[pl.BlockSpec(memory_space=pltpu.SMEM)] + [vmem] * 7,
        out_specs=[vmem] * 4,
        out_shape=[factor, factor, tower, tower],
        scratch_shapes=[pltpu.VMEM((experts, rows, width), F32)] * 2,
        cost_estimate=pl.CostEstimate(
            flops=2 * rows * experts_w.size, bytes_accessed=2 * experts_w.size, transcendentals=0
        ),
        compiler_params=pltpu.CompilerParams(vmem_limit_bytes=24 * 1024 * 1024),
    )(
        jnp.stack([part, group]).astype(jnp.int32),
        kept,
        taken,
        experts_w,
        gates_w.T,
        tower_w,
        tower_v,
        labels,
    )


def pack_kernel(
    own_rows_ref,
    other_rows_ref,
    mine_ref,
    theirs_ref,
    from_other_ref,
    tower_mine_ref,
    tower_theirs_ref,
    out_ref,
    rows_ref,
    factor_ref,
    tower_ref,
    block_ref,
):
    blocks, each, width = out_ref.shape
    count = mine_ref.shape[0]
    main_rows = each - 8
    down = (((0,), (0,)), ((), ()))
    rows_ref[: 2 * count] = own_rows_ref[...]
    rows_ref[2 * count :] = other_rows_ref[...]
    factor_ref[:count] = mine_ref[...]
    factor_ref[count : 2 * count] = from_other_ref[:count]
    factor_ref[2 * count : 3 * count] = theirs_ref[...]
    factor_ref[3 * count :] = from_other_ref[count:]
    tower_ref[...] = tower_mine_ref[...].astype(F32) + tower_theirs_ref[...].astype(F32)
    tower_rows = tower_ref.shape[0] - 16
    window = tower_rows // 2 // blocks
    gates = lax.dot_general(
        factor_ref[:, width:], rows_ref[...], down, preferred_element_type=F32
    )
    gate_count = GATE_STEPS * 8
    per_step = 8
    for step in range(blocks // per_step):
        at = step * per_step * main_rows
        main = lax.dot_general(
            rows_ref[:, at : at + per_step * main_rows],
            factor_ref[:, :width],
            down,
            preferred_element_type=F32,
        )
        for local in range(per_step):
            block = step * per_step + local
            block_ref[:main_rows] = main[local * main_rows : (local + 1) * main_rows]
            if block < gate_count:
                block_ref[main_rows : main_rows + 1] = gates[block : block + 1, :width]
                block_ref[main_rows + 1 : main_rows + 2] = gates[block : block + 1, width:]
            else:
                block_ref[main_rows : main_rows + 2] = jnp.zeros((2, width), F32)
            if block == gate_count:
                vectors = tower_ref[tower_rows:]
                half = width // 2
                block_ref[main_rows : main_rows + 1, :half] = vectors[0:1]
                block_ref[main_rows : main_rows + 1, half:] = vectors[1:2]
                block_ref[main_rows + 1 : main_rows + 2, :half] = vectors[2:3]
            low = tower_ref[block * window : (block + 1) * window]
            high = tower_ref[tower_rows // 2 + block * window : tower_rows // 2 + (block + 1) * window]
            block_ref[main_rows + 2 : main_rows + 2 + window, : width // 2] = low
            block_ref[main_rows + 2 : main_rows + 2 + window, width // 2 :] = high
            out_ref[block] = block_ref[...].astype(BF16)


def pack(own_rows, other_rows, mine, theirs, from_other, tower_mine, tower_theirs, blocks):
    count, features = own_rows.shape
    width = features // 2
    each = features // blocks + 8
    vmem = pl.BlockSpec(memory_space=pltpu.VMEM)
    return pl.pallas_call(
        pack_kernel,
        in_specs=[vmem] * 7,
        out_specs=vmem,
        out_shape=jax.ShapeDtypeStruct((blocks, each, width), BF16),
        scratch_shapes=[
            pltpu.VMEM((2 * count, features), BF16),
            pltpu.VMEM((2 * count, mine.shape[1]), BF16),
            pltpu.VMEM(tower_mine.shape, F32),
            pltpu.VMEM((each, width), F32),
        ],
        cost_estimate=pl.CostEstimate(
            flops=4 * count * features * width,
            bytes_accessed=2 * blocks * each * width,
            transcendentals=0,
        ),
        compiler_params=pltpu.CompilerParams(vmem_limit_bytes=24 * 1024 * 1024),
    )(own_rows, other_rows, mine, theirs, from_other, tower_mine, tower_theirs)


def on_device(
    teacher_rows,
    expert_ids,
    router,
    teacher_up,
    teacher_down,
    student_experts,
    student_gates,
    tower_in,
    tower_out,
    soft_labels,
    label_masks,
):
    rows_dev, feature_dim = teacher_rows.shape
    expert_total = lax.axis_size("ep")
    width_parts = lax.axis_size("mp")
    group_index = lax.axis_index("grp")
    chips = expert_total * width_parts
    capacity = 4 * rows_dev // expert_total
    chunk_slots = capacity // SLOT_CHUNKS

    labels = swap(jnp.concatenate([soft_labels, label_masks.astype(F32)], 1), "grp")

    experts = jnp.arange(expert_total, dtype=jnp.int32)
    hot = [(expert_ids[:, c : c + 1] == experts[None, :]) for c in range(2)]
    named = (hot[0] | hot[1]).astype(BF16)
    sample = jnp.arange(rows_dev, dtype=jnp.int32)
    before = (sample[None, :] < sample[:, None]).astype(BF16)
    earlier = jnp.dot(before, named, preferred_element_type=F32)
    slots = [jnp.sum(jnp.where(h, earlier, 0.0), 1, keepdims=True).astype(jnp.int32) for h in hot]

    def places(chunk):
        found = []
        for c in range(2):
            local = slots[c] - chunk * chunk_slots
            inside = (local >= 0) & (local < chunk_slots)
            found.append(jnp.where(inside, expert_ids[:, c : c + 1] * chunk_slots + local, -1))
        return found

    targets = [places(chunk) for chunk in range(SLOT_CHUNKS)]

    received = []
    for chunk in range(SLOT_CHUNKS):
        outgoing = dispatch(
            expert_ids.T, teacher_rows, expert_total, chunk_slots, chunk * chunk_slots
        )
        received.append(lax.all_to_all(outgoing, "ep", split_axis=0, concat_axis=0, tiled=True))

    logits = jnp.dot(teacher_rows, router, preferred_element_type=F32)
    chosen = [jnp.sum(jnp.where(h, logits, 0.0), 1, keepdims=True) for h in hot]
    sigs = [jax.nn.sigmoid(v) for v in chosen]
    weights = [v / (sigs[0] + sigs[1]) for v in sigs]

    up_proj = teacher_up[0]
    down_proj = teacher_down[0]
    part = lax.axis_index("mp")
    half_width = feature_dim // width_parts
    mixed = jnp.zeros((rows_dev, half_width), F32)
    wide_lane = jnp.arange(chips * chunk_slots, dtype=jnp.int32)[None, :]
    wide_expert = wide_lane // (width_parts * chunk_slots)
    wide_place = wide_expert * chunk_slots + wide_lane % chunk_slots
    for chunk in range(SLOT_CHUNKS):
        rows_in = received[chunk].reshape(expert_total * chunk_slots, feature_dim)
        inner = jax.nn.gelu(jnp.dot(rows_in, up_proj, preferred_element_type=F32)).astype(BF16)
        partial = jnp.dot(inner, down_proj, preferred_element_type=F32).astype(BF16)
        outgoing = partial.reshape(expert_total, chunk_slots, width_parts, half_width)
        outgoing = outgoing.transpose(0, 2, 1, 3).reshape(chips, chunk_slots, half_width)
        returned = lax.all_to_all(outgoing, CHIPS, split_axis=0, concat_axis=0, tiled=True)
        returned = returned.reshape(chips * chunk_slots, half_width)
        first, second = targets[chunk]
        share = jnp.where(wide_place == first, weights[0], 0.0) + jnp.where(
            wide_place == second, weights[1], 0.0
        )
        high = share.astype(BF16)
        low = (share - high.astype(F32)).astype(BF16)
        if chunk < SLOT_CHUNKS - 1:
            mixed = mixed + jnp.dot(high, returned, preferred_element_type=F32)
            mixed = mixed + jnp.dot(low, returned, preferred_element_type=F32)
        else:
            kept, given, both = combine(part, high, low, returned, mixed)

    taken = swap(given, "mp")
    other_both = swap(both, "grp")

    sample_total = rows_dev * lax.axis_size("grp") * expert_total
    mine, theirs, tower_mine, tower_theirs = student_grads(
        part,
        group_index,
        kept,
        taken,
        student_experts,
        student_gates,
        tower_in,
        tower_out,
        labels,
        1.0 / math.sqrt(sample_total),
    )
    theirs = swap(theirs, "grp")
    tower_theirs = swap(tower_theirs, "grp")
    from_other = swap(jnp.concatenate([mine, theirs], 0), "mp")
    packed = pack(
        both, other_both, mine, theirs, from_other, tower_mine, tower_theirs, expert_total
    )

    parts = lax.all_to_all(packed, "ep", split_axis=0, concat_axis=0, tiled=True)
    total = jnp.sum(parts.astype(F32), 0).astype(BF16)
    spread = jnp.broadcast_to(total[None], (chips,) + total.shape)
    own_half = lax.all_to_all(spread, CHIPS, split_axis=0, concat_axis=0, tiled=True)
    other_half = swap(own_half, "grp")
    filled = unpack(own_half, group_index, chips, width_parts, ())
    main, tower, gates, vector = unpack(other_half, 1 - group_index, chips, width_parts, filled)
    return (
        main.reshape(student_experts.shape),
        gates.reshape(-1, feature_dim).T,
        tower.reshape(tower_in.shape),
        vector.reshape(2, -1)[:, : tower_out.size // 2].reshape(tower_out.shape),
    )


def solution(mesh):
    return jax.shard_map(
        on_device,
        mesh=mesh,
        in_specs=(
            P(("grp", "ep"), None),
            P(("grp", "ep"), None),
            P(),
            P("ep", None, "mp"),
            P("ep", "mp", None),
            P(),
            P(),
            P(),
            P(),
            P(("grp", "ep", "mp"), None),
            P(("grp", "ep", "mp"), None),
        ),
        out_specs=(P(), P(), P(), P()),
        check_vma=False,
    )
```

```python
import functools
import math

import jax
import jax.numpy as jnp
from jax import lax
from jax.experimental import pallas as pl
from jax.experimental.pallas import tpu as pltpu
from jax.sharding import PartitionSpec as P

F32 = jnp.float32
BF16 = jnp.bfloat16
SLOT_CHUNKS = 2
CHIPS = ("ep", "mp")
GATE_STEPS = 3


def swap(shard, axis):
    return lax.ppermute(shard, axis, [(0, 1), (1, 0)])


def unpack_kernel(place_ref, half_ref, *refs):
    main_ref, tower_ref, gate_ref, vector_ref = refs[-4:]
    earlier_ref = refs[0] if len(refs) > 4 else None
    blocks, parts, _, width = half_ref.shape
    main_rows = main_ref.shape[1] // blocks
    tower_rows = tower_ref.shape[2] // blocks
    tower_width = tower_ref.shape[3]
    step = pl.program_id(0)
    for block in range(blocks):
        values = [half_ref[block, part].astype(F32) for part in range(parts)]
        for part in range(parts):
            main_ref[part, block * main_rows : (block + 1) * main_rows, :] = values[part][
                :main_rows
            ]
        tower = sum(value[main_rows + 2 : main_rows + 2 + tower_rows] for value in values)
        rows = slice(block * tower_rows, (block + 1) * tower_rows)
        tower_ref[0, 0, rows, :] = tower[:, :tower_width]
        tower_ref[0, 1, rows, :] = tower[:, tower_width:]
        rests = [value[main_rows : main_rows + 2] for value in values]

        @pl.when(step < GATE_STEPS)
        def _(rests=rests, block=block):
            for part in range(parts):
                for row in range(2):
                    at = (part * 2 + row) * width
                    gate_ref[0, block : block + 1, at : at + width] = rests[part][row : row + 1]

        if block == 0:

            @pl.when(step == GATE_STEPS)
            def _(rests=rests):
                vectors = sum(rests)
                pieces = [
                    vectors[0:1, : width // 2],
                    vectors[0:1, width // 2 :],
                    vectors[1:2, : width // 2],
                ]
                low = place_ref[0] == 0
                for i, value in enumerate(pieces):
                    for own, row in ((low, i), (jnp.logical_not(low), i + len(pieces))):
                        if earlier_ref is None:
                            vector_ref[row : row + 1] = value
                        else:
                            kept = earlier_ref[row : row + 1]
                            vector_ref[row : row + 1] = jnp.where(own, value, kept)


def unpack(half, place, chips, parts, filled):
    _, each, width = half.shape
    outer = chips // parts
    step_blocks = 8
    main_rows, tower_rows = each - 8, 6
    tower_width = width // 2
    out_shape = [
        jax.ShapeDtypeStruct((parts, outer * main_rows, 2 * width), F32),
        jax.ShapeDtypeStruct((2, 2, outer * tower_rows, tower_width), F32),
        jax.ShapeDtypeStruct((2, GATE_STEPS * step_blocks, 2 * parts * width), F32),
        jax.ShapeDtypeStruct((6, tower_width), F32),
    ]
    size = sum(4 * math.prod(shape.shape) for shape in out_shape) // 2 + 2 * half.size
    return pl.pallas_call(
        unpack_kernel,
        grid_spec=pltpu.PrefetchScalarGridSpec(
            num_scalar_prefetch=1,
            grid=(outer // step_blocks,),
            in_specs=[pl.BlockSpec((step_blocks, parts, each, width), lambda i, g: (i, 0, 0, 0))]
            + ([pl.BlockSpec((6, tower_width), lambda i, g: (0, 0))] if filled else [])
            + [pl.BlockSpec(memory_space=pl.ANY)] * (len(filled) - 1),
            out_specs=[
                pl.BlockSpec((parts, step_blocks * main_rows, width), lambda i, g: (0, i, g[0])),
                pl.BlockSpec(
                    (1, 2, step_blocks * tower_rows, tower_width), lambda i, g: (g[0], 0, i, 0)
                ),
                pl.BlockSpec(
                    (1, step_blocks, 2 * parts * width),
                    lambda i, g: (g[0], jnp.minimum(i, GATE_STEPS - 1), 0),
                ),
                pl.BlockSpec((6, tower_width), lambda i, g: (0, 0)),
            ],
        ),
        out_shape=out_shape,
        input_output_aliases={3 + i: i for i in range(len(filled) - 1)},
        cost_estimate=pl.CostEstimate(flops=half.size, bytes_accessed=size, transcendentals=0),
        compiler_params=pltpu.CompilerParams(vmem_limit_bytes=14 * 1024 * 1024),
    )(place.astype(jnp.int32).reshape(1), half.reshape(outer, parts, each, width), *filled[3:], *filled[:3])


def dispatch_kernel(ids_ref, rows_ref, out_ref, target_ref, *, experts, first_slot):
    step = pl.program_id(0)
    count = rows_ref.shape[0]
    block_experts, slots, _ = out_ref.shape

    @pl.when(step == 0)
    def _():
        ids = ids_ref[...]
        expert = lax.broadcasted_iota(jnp.int32, (experts, count), 0)
        hot = [expert == ids[c : c + 1] for c in range(2)]
        named = jnp.where(hot[0] | hot[1], 1.0, 0.0).astype(BF16)
        order = [lax.broadcasted_iota(jnp.int32, (count, count), d) for d in (0, 1)]
        before = jnp.where(order[0] < order[1], 1.0, 0.0).astype(BF16)
        earlier = jnp.dot(named, before, preferred_element_type=F32)
        for c in range(2):
            slot = jnp.sum(jnp.where(hot[c], earlier, 0.0), 0, keepdims=True).astype(jnp.int32)
            local = slot - first_slot
            inside = (local >= 0) & (local < slots)
            target_ref[c : c + 1, :] = jnp.where(inside, ids[c : c + 1] * slots + local, -1)

    block = block_experts * slots
    place = step * block + lax.broadcasted_iota(jnp.int32, (block, count), 0)
    chosen = (place == target_ref[0:1, :]) | (place == target_ref[1:2, :])
    pick = jnp.where(chosen, 1.0, 0.0).astype(BF16)
    rows = jnp.dot(pick, rows_ref[...], preferred_element_type=F32).astype(BF16)
    out_ref[...] = rows.reshape(out_ref.shape)


def dispatch(ids_by_choice, rows, experts, slots, first_slot):
    count, feature_dim = rows.shape
    block_experts = experts // 2
    return pl.pallas_call(
        functools.partial(dispatch_kernel, experts=experts, first_slot=first_slot),
        grid=(2,),
        in_specs=[
            pl.BlockSpec((2, count), lambda i: (0, 0)),
            pl.BlockSpec((count, feature_dim), lambda i: (0, 0)),
        ],
        out_specs=pl.BlockSpec((block_experts, slots, feature_dim), lambda i: (i, 0, 0)),
        out_shape=jax.ShapeDtypeStruct((experts, slots, feature_dim), BF16),
        scratch_shapes=[pltpu.VMEM((2, count), jnp.int32)],
        cost_estimate=pl.CostEstimate(
            flops=2 * experts * slots * rows.size,
            bytes_accessed=2 * rows.size + 2 * experts * slots * feature_dim,
            transcendentals=0,
        ),
        compiler_params=pltpu.CompilerParams(vmem_limit_bytes=56 * 1024 * 1024),
    )(ids_by_choice, rows)


def student_first_kernel(
    part_ref,
    kept_ref,
    experts_ref,
    gates_ref,
    tower_ref,
    pre_ref,
    logit_ref,
    experts_out_ref,
    gates_out_ref,
    tower_out_ref,
    own_ref,
    gates_own_ref,
    sems,
):
    half = kept_ref.shape[1]
    part = part_ref[0]
    own = pl.ds(pl.multiple_of(part * half, half), half)
    other = pl.ds(pl.multiple_of((1 - part) * half, half), half)
    copies = [
        pltpu.make_async_copy(experts_ref.at[own], own_ref, sems.at[0]),
        pltpu.make_async_copy(gates_ref.at[:, own], gates_own_ref, sems.at[1]),
        pltpu.make_async_copy(experts_ref.at[other], experts_out_ref, sems.at[2]),
        pltpu.make_async_copy(gates_ref.at[:, other], gates_out_ref, sems.at[3]),
        pltpu.make_async_copy(tower_ref, tower_out_ref, sems.at[4]),
    ]
    for copy in copies:
        copy.start()
    kept = kept_ref[...]
    copies[0].wait()
    pre_ref[...] = jnp.dot(kept, own_ref[...], preferred_element_type=F32)
    copies[1].wait()
    logit_ref[...] = lax.dot_general(
        kept, gates_own_ref[...], (((1,), (1,)), ((), ())), preferred_element_type=F32
    )
    for copy in copies[2:]:
        copy.wait()


def student_first(part, kept, experts_w, gates_t, tower_w):
    rows, half = kept.shape
    vmem = pl.BlockSpec(memory_space=pltpu.VMEM)
    anywhere = pl.BlockSpec(memory_space=pl.ANY)
    experts_half = (half, experts_w.shape[1])
    gates_half = (gates_t.shape[0], half)
    return pl.pallas_call(
        student_first_kernel,
        in_specs=[pl.BlockSpec(memory_space=pltpu.SMEM), vmem, anywhere, anywhere, anywhere],
        out_specs=[vmem] * 5,
        out_shape=[
            jax.ShapeDtypeStruct((rows, experts_w.shape[1]), F32),
            jax.ShapeDtypeStruct((rows, gates_t.shape[0]), F32),
            jax.ShapeDtypeStruct(experts_half, BF16),
            jax.ShapeDtypeStruct(gates_half, BF16),
            jax.ShapeDtypeStruct(tower_w.shape, BF16),
        ],
        scratch_shapes=[
            pltpu.VMEM(experts_half, BF16),
            pltpu.VMEM(gates_half, BF16),
            pltpu.SemaphoreType.DMA((5,)),
        ],
        cost_estimate=pl.CostEstimate(
            flops=rows * experts_w.size, bytes_accessed=2 * experts_w.size, transcendentals=0
        ),
        compiler_params=pltpu.CompilerParams(vmem_limit_bytes=14 * 1024 * 1024),
    )(part.reshape(1), kept, experts_w, gates_t, tower_w)


def student_kernel(
    group_ref,
    taken_ref,
    first_pre_ref,
    first_logit_ref,
    experts_ref,
    gates_ref,
    tower_in_ref,
    tower_out_ref,
    labels_ref,
    mine_ref,
    theirs_ref,
    tower_mine_ref,
    tower_theirs_ref,
    act_ref,
    slope_ref,
    *,
    loss_scale,
):
    tasks, width, tower_width = tower_in_ref.shape
    columns = gates_ref.shape[0]
    experts = columns // tasks
    group = group_ref[0]
    taken = taken_ref[...]
    across = (((1,), (1,)), ((), ()))
    down = (((0,), (0,)), ((), ()))

    logit = first_logit_ref[...] + lax.dot_general(
        taken, gates_ref[...], across, preferred_element_type=F32
    )
    sig = jax.nn.sigmoid(logit)
    task_of = [lax.broadcasted_iota(jnp.int32, (columns, columns), d) // experts for d in (0, 1)]
    same_task = jnp.where(task_of[0] == task_of[1], 1.0, 0.0)

    def task_sum(value):
        return jnp.dot(
            value, same_task, precision=lax.Precision.HIGHEST, preferred_element_type=F32
        )

    gate_sum = task_sum(sig)
    share = sig / gate_sum

    scale = math.sqrt(2.0 / math.pi)
    per_piece = 2
    for k in range(experts):
        if k % per_piece == 0:
            at = slice(k * width, (k + per_piece) * width)
            wide = first_pre_ref[:, at]
            wide += jnp.dot(taken, experts_ref[:, at], preferred_element_type=F32)
        pre = wide[:, k % per_piece * width : (k % per_piece + 1) * width]
        square = pre * pre
        tanh = jnp.tanh(scale * (pre + 0.044715 * (square * pre)))
        cdf = 0.5 * (1.0 + tanh)
        act_ref[k] = pre * cdf
        slope_ref[k] = cdf + (0.5 * scale) * pre * (1.0 - tanh * tanh) * (
            1.0 + (3 * 0.044715) * square
        )

    mix_grads, tower_in_grads = [], []
    lane = lax.broadcasted_iota(jnp.int32, share.shape, 1)
    share_grad = jnp.zeros(share.shape, F32)
    per_group = tasks // 2
    vector_rows = tower_mine_ref.shape[0] - per_group * width
    vector_row = lax.broadcasted_iota(jnp.int32, (vector_rows, tower_width), 0)
    vectors = [jnp.zeros((vector_rows, tower_width), F32)] * 2
    for t in range(tasks):
        mixture = jnp.zeros(act_ref.shape[1:], F32)
        for k in range(experts):
            column = t * experts + k
            mixture += share[:, column : column + 1] * act_ref[k]
        mixture = mixture.astype(BF16)
        tower_w = tower_in_ref[t]
        tower_pre = jnp.dot(mixture, tower_w, preferred_element_type=F32)
        tower_sig = jax.nn.sigmoid(tower_pre)
        tower_hid = tower_pre * tower_sig
        tower_vec = tower_out_ref[t : t + 1, :].astype(F32)
        task_logit = jnp.sum(tower_hid * tower_vec, 1, keepdims=True)
        mask = labels_ref[:, tasks + t : tasks + t + 1]
        error = jax.nn.sigmoid(task_logit) - labels_ref[:, t : t + 1]
        logit_grad = mask * error * loss_scale
        owner, local = t // per_group, t % per_group
        vectors[owner] = jnp.where(
            vector_row == local,
            jnp.sum(logit_grad * tower_hid, 0, keepdims=True),
            vectors[owner],
        )
        tower_grad = (
            (logit_grad * tower_vec) * tower_sig * (1.0 + tower_pre * (1.0 - tower_sig))
        ).astype(BF16)
        tower_in_grads.append(
            lax.dot_general(mixture, tower_grad, down, preferred_element_type=F32)
        )
        mix_grad = lax.dot_general(tower_grad, tower_w, across, preferred_element_type=F32)
        mix_grads.append(mix_grad)
        for k in range(experts):
            value = jnp.sum(mix_grad * act_ref[k], 1, keepdims=True)
            share_grad = jnp.where(lane == t * experts + k, value, share_grad)

    low_group = group == 0
    for local in range(per_group):
        at = slice(local * width, (local + 1) * width)
        low, high = tower_in_grads[local], tower_in_grads[local + per_group]
        tower_mine_ref[at] = jnp.where(low_group, low, high).astype(BF16)
        tower_theirs_ref[at] = jnp.where(low_group, high, low).astype(BF16)
    tower_mine_ref[per_group * width :] = jnp.where(low_group, vectors[0], vectors[1]).astype(BF16)
    tower_theirs_ref[per_group * width :] = jnp.where(low_group, vectors[1], vectors[0]).astype(
        BF16
    )

    def pre_grad(k):
        act_grad = jnp.zeros(act_ref.shape[1:], F32)
        for t in range(tasks):
            column = t * experts + k
            act_grad += share[:, column : column + 1] * mix_grads[t]
        return act_grad * slope_ref[k]

    for k in range(experts // 2):
        at = slice(k * width, (k + 1) * width)
        low, high = pre_grad(k), pre_grad(k + experts // 2)
        mine_ref[:, at] = jnp.where(low_group, low, high).astype(BF16)
        theirs_ref[:, at] = jnp.where(low_group, high, low).astype(BF16)

    sig_grad = (share_grad - task_sum(share * share_grad)) / gate_sum
    gate_grad = (sig_grad * sig * (1.0 - sig)).astype(BF16)
    end = experts // 2 * width
    lanes = mine_ref.shape[1] - end
    source = lax.broadcasted_iota(jnp.int32, (columns, lanes), 0)
    lane_at = lax.broadcasted_iota(jnp.int32, (columns, lanes), 1)
    for ref, owner in ((mine_ref, group), (theirs_ref, 1 - group)):
        wanted = (source == lane_at + owner * (columns // 2)) & (lane_at < columns // 2)
        move = jnp.where(wanted, 1.0, 0.0).astype(BF16)
        ref[:, end:] = jnp.dot(gate_grad, move, preferred_element_type=F32).astype(BF16)


def student_grads(group, taken, first_part, tower_v, labels, loss_scale):
    pre, _, _, _, tower_w = first_part
    rows, columns = pre.shape
    tasks, width, tower_width = tower_w.shape
    experts = columns // width
    vmem = pl.BlockSpec(memory_space=pltpu.VMEM)
    factor = jax.ShapeDtypeStruct((rows, columns // 2 + 128), BF16)
    tower = jax.ShapeDtypeStruct((tasks // 2 * width + 16, tower_width), BF16)
    return pl.pallas_call(
        functools.partial(student_kernel, loss_scale=loss_scale),
        in_specs=[pl.BlockSpec(memory_space=pltpu.SMEM)] + [vmem] * 8,
        out_specs=[vmem] * 4,
        out_shape=[factor, factor, tower, tower],
        scratch_shapes=[pltpu.VMEM((experts, rows, width), F32)] * 2,
        cost_estimate=pl.CostEstimate(
            flops=rows * taken.shape[1] * columns, bytes_accessed=4 * pre.size, transcendentals=0
        ),
        compiler_params=pltpu.CompilerParams(vmem_limit_bytes=14 * 1024 * 1024),
    )(group.reshape(1), taken, *first_part, tower_v, labels)


def pack_kernel(
    own_rows_ref,
    other_rows_ref,
    mine_ref,
    from_part_ref,
    theirs_ref,
    from_far_ref,
    tower_mine_ref,
    tower_theirs_ref,
    out_ref,
    rows_ref,
    factor_ref,
    tower_ref,
    block_ref,
):
    blocks, each, width = out_ref.shape
    count = mine_ref.shape[0]
    main_rows = each - 8
    down = (((0,), (0,)), ((), ()))
    rows_ref[: 2 * count] = own_rows_ref[...]
    rows_ref[2 * count :] = other_rows_ref[...]
    factor_ref[:count] = mine_ref[...]
    factor_ref[count : 2 * count] = from_part_ref[...]
    factor_ref[2 * count : 3 * count] = theirs_ref[...]
    factor_ref[3 * count :] = from_far_ref[...]
    tower_ref[...] = tower_mine_ref[...].astype(F32) + tower_theirs_ref[...].astype(F32)
    tower_rows = tower_ref.shape[0] - 16
    window = tower_rows // 2 // blocks
    gates = lax.dot_general(
        factor_ref[:, width:], rows_ref[...], down, preferred_element_type=F32
    )
    gate_count = GATE_STEPS * 8
    per_step = 8
    for step in range(blocks // per_step):
        at = step * per_step * main_rows
        main = lax.dot_general(
            rows_ref[:, at : at + per_step * main_rows],
            factor_ref[:, :width],
            down,
            preferred_element_type=F32,
        )
        for local in range(per_step):
            block = step * per_step + local
            block_ref[:main_rows] = main[local * main_rows : (local + 1) * main_rows]
            if block < gate_count:
                block_ref[main_rows : main_rows + 1] = gates[block : block + 1, :width]
                block_ref[main_rows + 1 : main_rows + 2] = gates[block : block + 1, width:]
            else:
                block_ref[main_rows : main_rows + 2] = jnp.zeros((2, width), F32)
            if block == gate_count:
                vectors = tower_ref[tower_rows:]
                half = width // 2
                block_ref[main_rows : main_rows + 1, :half] = vectors[0:1]
                block_ref[main_rows : main_rows + 1, half:] = vectors[1:2]
                block_ref[main_rows + 1 : main_rows + 2, :half] = vectors[2:3]
            low = tower_ref[block * window : (block + 1) * window]
            high = tower_ref[tower_rows // 2 + block * window : tower_rows // 2 + (block + 1) * window]
            block_ref[main_rows + 2 : main_rows + 2 + window, : width // 2] = low
            block_ref[main_rows + 2 : main_rows + 2 + window, width // 2 :] = high
            out_ref[block] = block_ref[...].astype(BF16)


def pack(own_rows, other_rows, mine, from_part, theirs, from_far, tower_mine, tower_theirs, blocks):
    count, features = own_rows.shape
    width = features // 2
    each = features // blocks + 8
    vmem = pl.BlockSpec(memory_space=pltpu.VMEM)
    return pl.pallas_call(
        pack_kernel,
        in_specs=[vmem] * 8,
        out_specs=vmem,
        out_shape=jax.ShapeDtypeStruct((blocks, each, width), BF16),
        scratch_shapes=[
            pltpu.VMEM((2 * count, features), BF16),
            pltpu.VMEM((2 * count, mine.shape[1]), BF16),
            pltpu.VMEM(tower_mine.shape, F32),
            pltpu.VMEM((each, width), F32),
        ],
        cost_estimate=pl.CostEstimate(
            flops=4 * count * features * width,
            bytes_accessed=2 * blocks * each * width,
            transcendentals=0,
        ),
        compiler_params=pltpu.CompilerParams(vmem_limit_bytes=14 * 1024 * 1024),
    )(own_rows, other_rows, mine, from_part, theirs, from_far, tower_mine, tower_theirs)


def on_device(
    teacher_rows,
    expert_ids,
    router,
    teacher_up,
    teacher_down,
    student_experts,
    student_gates,
    tower_in,
    tower_out,
    soft_labels,
    label_masks,
):
    rows_dev, feature_dim = teacher_rows.shape
    expert_total = lax.axis_size("ep")
    width_parts = lax.axis_size("mp")
    group_index = lax.axis_index("grp")
    chips = expert_total * width_parts
    capacity = 4 * rows_dev // expert_total
    chunk_slots = capacity // SLOT_CHUNKS

    labels = swap(jnp.concatenate([soft_labels, label_masks.astype(F32)], 1), "grp")

    experts = jnp.arange(expert_total, dtype=jnp.int32)
    hot = [(expert_ids[:, c : c + 1] == experts[None, :]) for c in range(2)]
    named = (hot[0] | hot[1]).astype(BF16)
    sample = jnp.arange(rows_dev, dtype=jnp.int32)
    before = (sample[None, :] < sample[:, None]).astype(BF16)
    earlier = jnp.dot(before, named, preferred_element_type=F32)
    slots = [jnp.sum(jnp.where(h, earlier, 0.0), 1, keepdims=True).astype(jnp.int32) for h in hot]

    def places(chunk):
        found = []
        for c in range(2):
            local = slots[c] - chunk * chunk_slots
            inside = (local >= 0) & (local < chunk_slots)
            found.append(jnp.where(inside, expert_ids[:, c : c + 1] * chunk_slots + local, -1))
        return found

    targets = [places(chunk) for chunk in range(SLOT_CHUNKS)]

    received = []
    for chunk in range(SLOT_CHUNKS):
        outgoing = dispatch(
            expert_ids.T, teacher_rows, expert_total, chunk_slots, chunk * chunk_slots
        )
        received.append(lax.all_to_all(outgoing, "ep", split_axis=0, concat_axis=0, tiled=True))

    logits = jnp.dot(teacher_rows, router, preferred_element_type=F32)
    chosen = [jnp.sum(jnp.where(h, logits, 0.0), 1, keepdims=True) for h in hot]
    sigs = [jax.nn.sigmoid(v) for v in chosen]
    weights = [v / (sigs[0] + sigs[1]) for v in sigs]

    up_proj = teacher_up[0]
    down_proj = teacher_down[0]
    part = lax.axis_index("mp")
    half_width = feature_dim // width_parts
    mixed = jnp.zeros((rows_dev, half_width), F32)
    wide_lane = jnp.arange(chips * chunk_slots, dtype=jnp.int32)[None, :]
    wide_expert = wide_lane // (width_parts * chunk_slots)
    wide_place = wide_expert * chunk_slots + wide_lane % chunk_slots
    for chunk in range(SLOT_CHUNKS):
        rows_in = received[chunk].reshape(expert_total * chunk_slots, feature_dim)
        inner = jax.nn.gelu(jnp.dot(rows_in, up_proj, preferred_element_type=F32)).astype(BF16)
        partial = jnp.dot(inner, down_proj, preferred_element_type=F32).astype(BF16)
        outgoing = partial.reshape(expert_total, chunk_slots, width_parts, half_width)
        outgoing = outgoing.transpose(0, 2, 1, 3).reshape(chips, chunk_slots, half_width)
        returned = lax.all_to_all(outgoing, CHIPS, split_axis=0, concat_axis=0, tiled=True)
        returned = returned.reshape(chips * chunk_slots, half_width)
        first, second = targets[chunk]
        share = jnp.where(wide_place == first, weights[0], 0.0) + jnp.where(
            wide_place == second, weights[1], 0.0
        )
        high = share.astype(BF16)
        low = (share - high.astype(F32)).astype(BF16)
        mixed = mixed + jnp.dot(high, returned, preferred_element_type=F32)
        mixed = mixed + jnp.dot(low, returned, preferred_element_type=F32)
    mixed = mixed.astype(BF16)

    half_rows = rows_dev // width_parts
    kept = lax.dynamic_slice_in_dim(mixed, part * half_rows, half_rows, 0)
    given = lax.dynamic_slice_in_dim(mixed, (1 - part) * half_rows, half_rows, 0)
    taken = swap(given, "mp")
    first_part = student_first(part, kept, student_experts, student_gates.T, tower_in)
    sample_total = rows_dev * lax.axis_size("grp") * expert_total
    mine, theirs, tower_mine, tower_theirs = student_grads(
        group_index, taken, first_part, tower_out, labels, 1.0 / math.sqrt(sample_total)
    )
    from_part = swap(mine, "mp")
    from_far = lax.ppermute(theirs, ("grp", "mp"), [(i, 3 - i) for i in range(4)])
    theirs = swap(theirs, "grp")
    tower_theirs = swap(tower_theirs, "grp")
    own_kept, own_given, mine = lax.optimization_barrier((kept, given, mine))
    both = jnp.concatenate([own_kept, own_given], 0)
    other_both = swap(both, "grp")
    packed = pack(
        both, other_both, mine, from_part, theirs, from_far, tower_mine, tower_theirs, expert_total
    )

    parts = lax.all_to_all(packed, "ep", split_axis=0, concat_axis=0, tiled=True)
    total = jnp.sum(parts.astype(F32), 0).astype(BF16)
    spread = jnp.broadcast_to(total[None], (chips,) + total.shape)
    own_half = lax.all_to_all(spread, CHIPS, split_axis=0, concat_axis=0, tiled=True)
    other_half = swap(own_half, "grp")
    filled = unpack(own_half, group_index, chips, width_parts, ())
    main, tower, gates, vector = unpack(other_half, 1 - group_index, chips, width_parts, filled)
    return (
        main.reshape(student_experts.shape),
        gates.reshape(-1, feature_dim).T,
        tower.reshape(tower_in.shape),
        vector,
    )


def solution(mesh):
    return jax.shard_map(
        on_device,
        mesh=mesh,
        in_specs=(
            P(("grp", "ep"), None),
            P(("grp", "ep"), None),
            P(),
            P("ep", None, "mp"),
            P("ep", "mp", None),
            P(),
            P(),
            P(),
            P(),
            P(("grp", "ep", "mp"), None),
            P(("grp", "ep", "mp"), None),
        ),
        out_specs=(P(), P(), P(), P()),
        check_vma=False,
    )
```

```python
import functools
import math

import jax
import jax.numpy as jnp
from jax import lax
from jax.experimental import pallas as pl
from jax.experimental.pallas import tpu as pltpu
from jax.sharding import PartitionSpec as P

F32 = jnp.float32
BF16 = jnp.bfloat16
SLOT_CHUNKS = 2
CHIPS = ("ep", "mp")
GATE_STEPS = 3


def swap(shard, axis):
    return lax.ppermute(shard, axis, [(0, 1), (1, 0)])


def unpack_kernel(place_ref, half_ref, *refs):
    main_ref, tower_ref, gate_ref, vector_ref = refs[-4:]
    earlier_ref = refs[0] if len(refs) > 4 else None
    _, parts, _, width = half_ref.shape
    blocks = gate_ref.shape[1]
    main_rows = main_ref.shape[1] // blocks
    tower_rows = tower_ref.shape[2] // blocks
    tower_width = tower_ref.shape[3]
    step = pl.program_id(0)
    for block in range(blocks):
        values = [half_ref[step * blocks + block, part].astype(F32) for part in range(parts)]
        for part in range(parts):
            main_ref[part, block * main_rows : (block + 1) * main_rows, :] = values[part][
                :main_rows
            ]
        tower = sum(value[main_rows + 2 : main_rows + 2 + tower_rows] for value in values)
        rows = slice(block * tower_rows, (block + 1) * tower_rows)
        tower_ref[0, 0, rows, :] = tower[:, :tower_width]
        tower_ref[0, 1, rows, :] = tower[:, tower_width:]
        rests = [value[main_rows : main_rows + 2] for value in values]

        @pl.when(step < GATE_STEPS)
        def _(rests=rests, block=block):
            for part in range(parts):
                for row in range(2):
                    at = (part * 2 + row) * width
                    gate_ref[0, block : block + 1, at : at + width] = rests[part][row : row + 1]

        if block == 0:

            @pl.when(step == GATE_STEPS)
            def _(rests=rests):
                vectors = sum(rests)
                pieces = [
                    vectors[0:1, : width // 2],
                    vectors[0:1, width // 2 :],
                    vectors[1:2, : width // 2],
                ]
                low = place_ref[0] == 0
                for i, value in enumerate(pieces):
                    for own, row in ((low, i), (jnp.logical_not(low), i + len(pieces))):
                        if earlier_ref is None:
                            vector_ref[row : row + 1] = value
                        else:
                            kept = earlier_ref[row : row + 1]
                            vector_ref[row : row + 1] = jnp.where(own, value, kept)


def unpack(half, place, chips, parts, filled):
    _, each, width = half.shape
    outer = chips // parts
    step_blocks = 8
    main_rows, tower_rows = each - 8, 6
    tower_width = width // 2
    out_shape = [
        jax.ShapeDtypeStruct((parts, outer * main_rows, 2 * width), F32),
        jax.ShapeDtypeStruct((2, 2, outer * tower_rows, tower_width), F32),
        jax.ShapeDtypeStruct((2, GATE_STEPS * step_blocks, 2 * parts * width), F32),
        jax.ShapeDtypeStruct((6, tower_width), F32),
    ]
    size = sum(4 * math.prod(shape.shape) for shape in out_shape) // 2 + 2 * half.size
    return pl.pallas_call(
        unpack_kernel,
        grid_spec=pltpu.PrefetchScalarGridSpec(
            num_scalar_prefetch=1,
            grid=(outer // step_blocks,),
            in_specs=[pl.BlockSpec(memory_space=pltpu.VMEM)]
            + ([pl.BlockSpec((6, tower_width), lambda i, g: (0, 0))] if filled else [])
            + [pl.BlockSpec(memory_space=pl.ANY)] * (len(filled) - 1),
            out_specs=[
                pl.BlockSpec((parts, step_blocks * main_rows, width), lambda i, g: (0, i, g[0])),
                pl.BlockSpec(
                    (1, 2, step_blocks * tower_rows, tower_width), lambda i, g: (g[0], 0, i, 0)
                ),
                pl.BlockSpec(
                    (1, step_blocks, 2 * parts * width),
                    lambda i, g: (g[0], jnp.minimum(i, GATE_STEPS - 1), 0),
                ),
                pl.BlockSpec((6, tower_width), lambda i, g: (0, 0)),
            ],
        ),
        out_shape=out_shape,
        input_output_aliases={3 + i: i for i in range(len(filled) - 1)},
        cost_estimate=pl.CostEstimate(flops=half.size, bytes_accessed=size, transcendentals=0),
        compiler_params=pltpu.CompilerParams(vmem_limit_bytes=14 * 1024 * 1024),
    )(place.astype(jnp.int32).reshape(1), half.reshape(outer, parts, each, width), *filled[3:], *filled[:3])


def dispatch_kernel(ids_ref, rows_ref, out_ref, target_ref, *, experts, first_slot):
    step = pl.program_id(0)
    count = rows_ref.shape[0]
    block_experts, slots, _ = out_ref.shape

    @pl.when(step == 0)
    def _():
        ids = ids_ref[...]
        expert = lax.broadcasted_iota(jnp.int32, (experts, count), 0)
        hot = [expert == ids[c : c + 1] for c in range(2)]
        named = jnp.where(hot[0] | hot[1], 1.0, 0.0).astype(BF16)
        order = [lax.broadcasted_iota(jnp.int32, (count, count), d) for d in (0, 1)]
        before = jnp.where(order[0] < order[1], 1.0, 0.0).astype(BF16)
        earlier = jnp.dot(named, before, preferred_element_type=F32)
        for c in range(2):
            slot = jnp.sum(jnp.where(hot[c], earlier, 0.0), 0, keepdims=True).astype(jnp.int32)
            local = slot - first_slot
            inside = (local >= 0) & (local < slots)
            target_ref[c : c + 1, :] = jnp.where(inside, ids[c : c + 1] * slots + local, -1)

    block = block_experts * slots
    place = step * block + lax.broadcasted_iota(jnp.int32, (block, count), 0)
    chosen = (place == target_ref[0:1, :]) | (place == target_ref[1:2, :])
    pick = jnp.where(chosen, 1.0, 0.0).astype(BF16)
    rows = jnp.dot(pick, rows_ref[...], preferred_element_type=F32).astype(BF16)
    out_ref[...] = rows.reshape(out_ref.shape)


def dispatch(ids_by_choice, rows, experts, slots, first_slot):
    count, feature_dim = rows.shape
    block_experts = experts // 2
    return pl.pallas_call(
        functools.partial(dispatch_kernel, experts=experts, first_slot=first_slot),
        grid=(2,),
        in_specs=[
            pl.BlockSpec((2, count), lambda i: (0, 0)),
            pl.BlockSpec((count, feature_dim), lambda i: (0, 0)),
        ],
        out_specs=pl.BlockSpec((block_experts, slots, feature_dim), lambda i: (i, 0, 0)),
        out_shape=jax.ShapeDtypeStruct((experts, slots, feature_dim), BF16),
        scratch_shapes=[pltpu.VMEM((2, count), jnp.int32)],
        cost_estimate=pl.CostEstimate(
            flops=2 * experts * slots * rows.size,
            bytes_accessed=2 * rows.size + 2 * experts * slots * feature_dim,
            transcendentals=0,
        ),
        compiler_params=pltpu.CompilerParams(vmem_limit_bytes=56 * 1024 * 1024),
    )(ids_by_choice, rows)


def student_first_kernel(
    part_ref,
    kept_ref,
    experts_ref,
    gates_ref,
    tower_ref,
    pre_ref,
    logit_ref,
    experts_out_ref,
    gates_out_ref,
    tower_out_ref,
    own_ref,
    gates_own_ref,
    sems,
):
    half = kept_ref.shape[1]
    part = part_ref[0]
    own = pl.ds(pl.multiple_of(part * half, half), half)
    other = pl.ds(pl.multiple_of((1 - part) * half, half), half)
    copies = [
        pltpu.make_async_copy(experts_ref.at[own], own_ref, sems.at[0]),
        pltpu.make_async_copy(gates_ref.at[:, own], gates_own_ref, sems.at[1]),
        pltpu.make_async_copy(experts_ref.at[other], experts_out_ref, sems.at[2]),
        pltpu.make_async_copy(gates_ref.at[:, other], gates_out_ref, sems.at[3]),
        pltpu.make_async_copy(tower_ref, tower_out_ref, sems.at[4]),
    ]
    for copy in copies:
        copy.start()
    kept = kept_ref[...]
    copies[0].wait()
    pre_ref[...] = jnp.dot(kept, own_ref[...], preferred_element_type=F32)
    copies[1].wait()
    logit_ref[...] = lax.dot_general(
        kept, gates_own_ref[...], (((1,), (1,)), ((), ())), preferred_element_type=F32
    )
    for copy in copies[2:]:
        copy.wait()


def student_first(part, kept, experts_w, gates_t, tower_w):
    rows, half = kept.shape
    vmem = pl.BlockSpec(memory_space=pltpu.VMEM)
    anywhere = pl.BlockSpec(memory_space=pl.ANY)
    experts_half = (half, experts_w.shape[1])
    gates_half = (gates_t.shape[0], half)
    return pl.pallas_call(
        student_first_kernel,
        in_specs=[pl.BlockSpec(memory_space=pltpu.SMEM), vmem, anywhere, anywhere, anywhere],
        out_specs=[vmem] * 5,
        out_shape=[
            jax.ShapeDtypeStruct((rows, experts_w.shape[1]), F32),
            jax.ShapeDtypeStruct((rows, gates_t.shape[0]), F32),
            jax.ShapeDtypeStruct(experts_half, BF16),
            jax.ShapeDtypeStruct(gates_half, BF16),
            jax.ShapeDtypeStruct(tower_w.shape, BF16),
        ],
        scratch_shapes=[
            pltpu.VMEM(experts_half, BF16),
            pltpu.VMEM(gates_half, BF16),
            pltpu.SemaphoreType.DMA((5,)),
        ],
        cost_estimate=pl.CostEstimate(
            flops=rows * experts_w.size, bytes_accessed=2 * experts_w.size, transcendentals=0
        ),
        compiler_params=pltpu.CompilerParams(vmem_limit_bytes=14 * 1024 * 1024),
    )(part.reshape(1), kept, experts_w, gates_t, tower_w)


def student_kernel(
    group_ref,
    taken_ref,
    first_pre_ref,
    first_logit_ref,
    experts_ref,
    gates_ref,
    tower_in_ref,
    tower_out_ref,
    labels_ref,
    mine_ref,
    theirs_ref,
    tower_mine_ref,
    tower_theirs_ref,
    act_ref,
    slope_ref,
    *,
    loss_scale,
):
    tasks, width, tower_width = tower_in_ref.shape
    columns = gates_ref.shape[0]
    experts = columns // tasks
    group = group_ref[0]
    taken = taken_ref[...]
    across = (((1,), (1,)), ((), ()))
    down = (((0,), (0,)), ((), ()))

    logit = first_logit_ref[...] + lax.dot_general(
        taken, gates_ref[...], across, preferred_element_type=F32
    )
    sig = jax.nn.sigmoid(logit)
    task_of = [lax.broadcasted_iota(jnp.int32, (columns, columns), d) // experts for d in (0, 1)]
    same_task = jnp.where(task_of[0] == task_of[1], 1.0, 0.0)

    def task_sum(value):
        return jnp.dot(
            value, same_task, precision=lax.Precision.HIGHEST, preferred_element_type=F32
        )

    gate_sum = task_sum(sig)
    share = sig / gate_sum

    scale = math.sqrt(2.0 / math.pi)
    per_piece = 2
    for k in range(experts):
        if k % per_piece == 0:
            at = slice(k * width, (k + per_piece) * width)
            wide = first_pre_ref[:, at]
            wide += jnp.dot(taken, experts_ref[:, at], preferred_element_type=F32)
        pre = wide[:, k % per_piece * width : (k % per_piece + 1) * width]
        square = pre * pre
        tanh = jnp.tanh(scale * (pre + 0.044715 * (square * pre)))
        cdf = 0.5 * (1.0 + tanh)
        act_ref[k] = pre * cdf
        slope_ref[k] = cdf + (0.5 * scale) * pre * (1.0 - tanh * tanh) * (
            1.0 + (3 * 0.044715) * square
        )

    mix_grads, tower_in_grads = [], []
    lane = lax.broadcasted_iota(jnp.int32, share.shape, 1)
    share_grad = jnp.zeros(share.shape, F32)
    per_group = tasks // 2
    vector_rows = tower_mine_ref.shape[0] - per_group * width
    vector_row = lax.broadcasted_iota(jnp.int32, (vector_rows, tower_width), 0)
    vectors = [jnp.zeros((vector_rows, tower_width), F32)] * 2
    for t in range(tasks):
        mixture = jnp.zeros(act_ref.shape[1:], F32)
        for k in range(experts):
            column = t * experts + k
            mixture += share[:, column : column + 1] * act_ref[k]
        mixture = mixture.astype(BF16)
        tower_w = tower_in_ref[t]
        tower_pre = jnp.dot(mixture, tower_w, preferred_element_type=F32)
        tower_sig = jax.nn.sigmoid(tower_pre)
        tower_hid = tower_pre * tower_sig
        tower_vec = tower_out_ref[t : t + 1, :].astype(F32)
        task_logit = jnp.sum(tower_hid * tower_vec, 1, keepdims=True)
        mask = labels_ref[:, tasks + t : tasks + t + 1]
        error = jax.nn.sigmoid(task_logit) - labels_ref[:, t : t + 1]
        logit_grad = mask * error * loss_scale
        owner, local = t // per_group, t % per_group
        vectors[owner] = jnp.where(
            vector_row == local,
            jnp.sum(logit_grad * tower_hid, 0, keepdims=True),
            vectors[owner],
        )
        tower_grad = (
            (logit_grad * tower_vec) * tower_sig * (1.0 + tower_pre * (1.0 - tower_sig))
        ).astype(BF16)
        tower_in_grads.append(
            lax.dot_general(mixture, tower_grad, down, preferred_element_type=F32)
        )
        mix_grad = lax.dot_general(tower_grad, tower_w, across, preferred_element_type=F32)
        mix_grads.append(mix_grad)
        for k in range(experts):
            value = jnp.sum(mix_grad * act_ref[k], 1, keepdims=True)
            share_grad = jnp.where(lane == t * experts + k, value, share_grad)

    low_group = group == 0
    for local in range(per_group):
        at = slice(local * width, (local + 1) * width)
        low, high = tower_in_grads[local], tower_in_grads[local + per_group]
        tower_mine_ref[at] = jnp.where(low_group, low, high).astype(BF16)
        tower_theirs_ref[at] = jnp.where(low_group, high, low).astype(BF16)
    tower_mine_ref[per_group * width :] = jnp.where(low_group, vectors[0], vectors[1]).astype(BF16)
    tower_theirs_ref[per_group * width :] = jnp.where(low_group, vectors[1], vectors[0]).astype(
        BF16
    )

    def pre_grad(k):
        act_grad = jnp.zeros(act_ref.shape[1:], F32)
        for t in range(tasks):
            column = t * experts + k
            act_grad += share[:, column : column + 1] * mix_grads[t]
        return act_grad * slope_ref[k]

    for k in range(experts // 2):
        at = slice(k * width, (k + 1) * width)
        low, high = pre_grad(k), pre_grad(k + experts // 2)
        mine_ref[:, at] = jnp.where(low_group, low, high).astype(BF16)
        theirs_ref[:, at] = jnp.where(low_group, high, low).astype(BF16)

    sig_grad = (share_grad - task_sum(share * share_grad)) / gate_sum
    gate_grad = (sig_grad * sig * (1.0 - sig)).astype(BF16)
    end = experts // 2 * width
    lanes = mine_ref.shape[1] - end
    source = lax.broadcasted_iota(jnp.int32, (columns, lanes), 0)
    lane_at = lax.broadcasted_iota(jnp.int32, (columns, lanes), 1)
    for ref, owner in ((mine_ref, group), (theirs_ref, 1 - group)):
        wanted = (source == lane_at + owner * (columns // 2)) & (lane_at < columns // 2)
        move = jnp.where(wanted, 1.0, 0.0).astype(BF16)
        ref[:, end:] = jnp.dot(gate_grad, move, preferred_element_type=F32).astype(BF16)


def student_grads(group, taken, first_part, tower_v, labels, loss_scale):
    pre, _, _, _, tower_w = first_part
    rows, columns = pre.shape
    tasks, width, tower_width = tower_w.shape
    experts = columns // width
    vmem = pl.BlockSpec(memory_space=pltpu.VMEM)
    factor = jax.ShapeDtypeStruct((rows, columns // 2 + 128), BF16)
    tower = jax.ShapeDtypeStruct((tasks // 2 * width + 16, tower_width), BF16)
    return pl.pallas_call(
        functools.partial(student_kernel, loss_scale=loss_scale),
        in_specs=[pl.BlockSpec(memory_space=pltpu.SMEM)] + [vmem] * 8,
        out_specs=[vmem] * 4,
        out_shape=[factor, factor, tower, tower],
        scratch_shapes=[pltpu.VMEM((experts, rows, width), F32)] * 2,
        cost_estimate=pl.CostEstimate(
            flops=rows * taken.shape[1] * columns, bytes_accessed=4 * pre.size, transcendentals=0
        ),
        compiler_params=pltpu.CompilerParams(vmem_limit_bytes=14 * 1024 * 1024),
    )(group.reshape(1), taken, *first_part, tower_v, labels)


def pack_kernel(
    own_rows_ref,
    other_rows_ref,
    mine_ref,
    from_part_ref,
    theirs_ref,
    from_far_ref,
    tower_mine_ref,
    tower_theirs_ref,
    out_ref,
    rows_ref,
    factor_ref,
    tower_ref,
    block_ref,
):
    blocks, each, width = out_ref.shape
    count = mine_ref.shape[0]
    main_rows = each - 8
    down = (((0,), (0,)), ((), ()))
    rows_ref[: 2 * count] = own_rows_ref[...]
    rows_ref[2 * count :] = other_rows_ref[...]
    factor_ref[:count] = mine_ref[...]
    factor_ref[count : 2 * count] = from_part_ref[...]
    factor_ref[2 * count : 3 * count] = theirs_ref[...]
    factor_ref[3 * count :] = from_far_ref[...]
    tower_ref[...] = tower_mine_ref[...].astype(F32) + tower_theirs_ref[...].astype(F32)
    tower_rows = tower_ref.shape[0] - 16
    window = tower_rows // 2 // blocks
    gates = lax.dot_general(
        factor_ref[:, width:], rows_ref[...], down, preferred_element_type=F32
    )
    gate_count = GATE_STEPS * 8
    per_step = 8
    for step in range(blocks // per_step):
        at = step * per_step * main_rows
        main = lax.dot_general(
            rows_ref[:, at : at + per_step * main_rows],
            factor_ref[:, :width],
            down,
            preferred_element_type=F32,
        )
        for local in range(per_step):
            block = step * per_step + local
            block_ref[:main_rows] = main[local * main_rows : (local + 1) * main_rows]
            if block < gate_count:
                block_ref[main_rows : main_rows + 1] = gates[block : block + 1, :width]
                block_ref[main_rows + 1 : main_rows + 2] = gates[block : block + 1, width:]
            else:
                block_ref[main_rows : main_rows + 2] = jnp.zeros((2, width), F32)
            if block == gate_count:
                vectors = tower_ref[tower_rows:]
                half = width // 2
                block_ref[main_rows : main_rows + 1, :half] = vectors[0:1]
                block_ref[main_rows : main_rows + 1, half:] = vectors[1:2]
                block_ref[main_rows + 1 : main_rows + 2, :half] = vectors[2:3]
            low = tower_ref[block * window : (block + 1) * window]
            high = tower_ref[tower_rows // 2 + block * window : tower_rows // 2 + (block + 1) * window]
            block_ref[main_rows + 2 : main_rows + 2 + window, : width // 2] = low
            block_ref[main_rows + 2 : main_rows + 2 + window, width // 2 :] = high
            out_ref[block] = block_ref[...].astype(BF16)


def pack(own_rows, other_rows, mine, from_part, theirs, from_far, tower_mine, tower_theirs, blocks):
    count, features = own_rows.shape
    width = features // 2
    each = features // blocks + 8
    vmem = pl.BlockSpec(memory_space=pltpu.VMEM)
    return pl.pallas_call(
        pack_kernel,
        in_specs=[vmem] * 8,
        out_specs=vmem,
        out_shape=jax.ShapeDtypeStruct((blocks, each, width), BF16),
        scratch_shapes=[
            pltpu.VMEM((2 * count, features), BF16),
            pltpu.VMEM((2 * count, mine.shape[1]), BF16),
            pltpu.VMEM(tower_mine.shape, F32),
            pltpu.VMEM((each, width), F32),
        ],
        cost_estimate=pl.CostEstimate(
            flops=4 * count * features * width,
            bytes_accessed=2 * blocks * each * width,
            transcendentals=0,
        ),
        compiler_params=pltpu.CompilerParams(vmem_limit_bytes=14 * 1024 * 1024),
    )(own_rows, other_rows, mine, from_part, theirs, from_far, tower_mine, tower_theirs)


def on_device(
    teacher_rows,
    expert_ids,
    router,
    teacher_up,
    teacher_down,
    student_experts,
    student_gates,
    tower_in,
    tower_out,
    soft_labels,
    label_masks,
):
    rows_dev, feature_dim = teacher_rows.shape
    expert_total = lax.axis_size("ep")
    width_parts = lax.axis_size("mp")
    group_index = lax.axis_index("grp")
    chips = expert_total * width_parts
    capacity = 4 * rows_dev // expert_total
    chunk_slots = capacity // SLOT_CHUNKS

    labels = swap(jnp.concatenate([soft_labels, label_masks.astype(F32)], 1), "grp")

    experts = jnp.arange(expert_total, dtype=jnp.int32)
    hot = [(expert_ids[:, c : c + 1] == experts[None, :]) for c in range(2)]
    named = (hot[0] | hot[1]).astype(BF16)
    sample = jnp.arange(rows_dev, dtype=jnp.int32)
    before = (sample[None, :] < sample[:, None]).astype(BF16)
    earlier = jnp.dot(before, named, preferred_element_type=F32)
    slots = [jnp.sum(jnp.where(h, earlier, 0.0), 1, keepdims=True).astype(jnp.int32) for h in hot]

    def places(chunk):
        found = []
        for c in range(2):
            local = slots[c] - chunk * chunk_slots
            inside = (local >= 0) & (local < chunk_slots)
            found.append(jnp.where(inside, expert_ids[:, c : c + 1] * chunk_slots + local, -1))
        return found

    targets = [places(chunk) for chunk in range(SLOT_CHUNKS)]

    received = []
    for chunk in range(SLOT_CHUNKS):
        outgoing = dispatch(
            expert_ids.T, teacher_rows, expert_total, chunk_slots, chunk * chunk_slots
        )
        received.append(lax.all_to_all(outgoing, "ep", split_axis=0, concat_axis=0, tiled=True))

    logits = jnp.dot(teacher_rows, router, preferred_element_type=F32)
    chosen = [jnp.sum(jnp.where(h, logits, 0.0), 1, keepdims=True) for h in hot]
    sigs = [jax.nn.sigmoid(v) for v in chosen]
    weights = [v / (sigs[0] + sigs[1]) for v in sigs]

    up_proj = teacher_up[0]
    down_proj = teacher_down[0]
    part = lax.axis_index("mp")
    half_width = feature_dim // width_parts
    mixed = jnp.zeros((rows_dev, half_width), F32)
    wide_lane = jnp.arange(chips * chunk_slots, dtype=jnp.int32)[None, :]
    wide_expert = wide_lane // (width_parts * chunk_slots)
    wide_place = wide_expert * chunk_slots + wide_lane % chunk_slots
    for chunk in range(SLOT_CHUNKS):
        rows_in = received[chunk].reshape(expert_total * chunk_slots, feature_dim)
        inner = jax.nn.gelu(jnp.dot(rows_in, up_proj, preferred_element_type=F32)).astype(BF16)
        partial = jnp.dot(inner, down_proj, preferred_element_type=F32).astype(BF16)
        outgoing = partial.reshape(expert_total, chunk_slots, width_parts, half_width)
        outgoing = outgoing.transpose(0, 2, 1, 3).reshape(chips, chunk_slots, half_width)
        returned = lax.all_to_all(outgoing, CHIPS, split_axis=0, concat_axis=0, tiled=True)
        returned = returned.reshape(chips * chunk_slots, half_width)
        first, second = targets[chunk]
        share = jnp.where(wide_place == first, weights[0], 0.0) + jnp.where(
            wide_place == second, weights[1], 0.0
        )
        mixed = mixed + jnp.dot(share.astype(BF16), returned, preferred_element_type=F32)
    mixed = mixed.astype(BF16)

    half_rows = rows_dev // width_parts
    kept = lax.dynamic_slice_in_dim(mixed, part * half_rows, half_rows, 0)
    given = lax.dynamic_slice_in_dim(mixed, (1 - part) * half_rows, half_rows, 0)
    taken = swap(given, "mp")
    first_part = student_first(part, kept, student_experts, student_gates.T, tower_in)
    sample_total = rows_dev * lax.axis_size("grp") * expert_total
    mine, theirs, tower_mine, tower_theirs = student_grads(
        group_index, taken, first_part, tower_out, labels, 1.0 / math.sqrt(sample_total)
    )
    from_part = swap(mine, "mp")
    from_far = lax.ppermute(theirs, ("grp", "mp"), [(i, 3 - i) for i in range(4)])
    theirs = swap(theirs, "grp")
    tower_theirs = swap(tower_theirs, "grp")
    own_kept, own_given, mine = lax.optimization_barrier((kept, given, mine))
    both = jnp.concatenate([own_kept, own_given], 0)
    other_both = swap(both, "grp")
    packed = pack(
        both, other_both, mine, from_part, theirs, from_far, tower_mine, tower_theirs, expert_total
    )

    parts = lax.all_to_all(packed, "ep", split_axis=0, concat_axis=0, tiled=True)
    total = jnp.sum(parts.astype(F32), 0).astype(BF16)
    spread = jnp.broadcast_to(total[None], (chips,) + total.shape)
    own_half = lax.all_to_all(spread, CHIPS, split_axis=0, concat_axis=0, tiled=True)
    other_half = swap(own_half, "grp")
    filled = unpack(own_half, group_index, chips, width_parts, ())
    main, tower, gates, vector = unpack(other_half, 1 - group_index, chips, width_parts, filled)
    return (
        main.reshape(student_experts.shape),
        gates.reshape(-1, feature_dim).T,
        tower.reshape(tower_in.shape),
        vector,
    )


def solution(mesh):
    return jax.shard_map(
        on_device,
        mesh=mesh,
        in_specs=(
            P(("grp", "ep"), None),
            P(("grp", "ep"), None),
            P(),
            P("ep", None, "mp"),
            P("ep", "mp", None),
            P(),
            P(),
            P(),
            P(),
            P(("grp", "ep", "mp"), None),
            P(("grp", "ep", "mp"), None),
        ),
        out_specs=(P(), P(), P(), P()),
        check_vma=False,
    )
```

```python
import functools
import math

import jax
import jax.numpy as jnp
from jax import lax
from jax.experimental import pallas as pl
from jax.experimental.pallas import tpu as pltpu
from jax.sharding import PartitionSpec as P

F32 = jnp.float32
BF16 = jnp.bfloat16
SLOT_CHUNKS = 2
CHIPS = ("mp", "ep")
GATE_STEPS = 3


def swap(shard, axis):
    return lax.ppermute(shard, axis, [(0, 1), (1, 0)])


def unpack_kernel(place_ref, half_ref, *refs):
    main_ref, tower_ref, gate_ref, vector_ref = refs[-4:]
    earlier_ref = refs[0] if len(refs) > 4 else None
    parts, _, _, width = half_ref.shape
    blocks = gate_ref.shape[1]
    main_rows = main_ref.shape[1] // blocks
    tower_rows = tower_ref.shape[2] // blocks
    tower_width = tower_ref.shape[3]
    step = pl.program_id(0)
    for block in range(blocks):
        values = [half_ref[part, step * blocks + block].astype(F32) for part in range(parts)]
        for part in range(parts):
            main_ref[part, block * main_rows : (block + 1) * main_rows, :] = values[part][
                :main_rows
            ]
        tower = sum(value[main_rows + 2 : main_rows + 2 + tower_rows] for value in values)
        rows = slice(block * tower_rows, (block + 1) * tower_rows)
        tower_ref[0, 0, rows, :] = tower[:, :tower_width]
        tower_ref[0, 1, rows, :] = tower[:, tower_width:]
        rests = [value[main_rows : main_rows + 2] for value in values]

        @pl.when(step < GATE_STEPS)
        def _(rests=rests, block=block):
            for part in range(parts):
                for row in range(2):
                    at = (part * 2 + row) * width
                    gate_ref[0, block : block + 1, at : at + width] = rests[part][row : row + 1]

        if block == 0:

            @pl.when(step == GATE_STEPS)
            def _(rests=rests):
                vectors = sum(rests)
                pieces = [
                    vectors[0:1, : width // 2],
                    vectors[0:1, width // 2 :],
                    vectors[1:2, : width // 2],
                ]
                low = place_ref[0] == 0
                for i, value in enumerate(pieces):
                    for own, row in ((low, i), (jnp.logical_not(low), i + len(pieces))):
                        if earlier_ref is None:
                            vector_ref[row : row + 1] = value
                        else:
                            kept = earlier_ref[row : row + 1]
                            vector_ref[row : row + 1] = jnp.where(own, value, kept)


def unpack(half, place, chips, parts, filled):
    _, each, width = half.shape
    outer = chips // parts
    step_blocks = 8
    main_rows, tower_rows = each - 8, 6
    tower_width = width // 2
    out_shape = [
        jax.ShapeDtypeStruct((parts, outer * main_rows, 2 * width), F32),
        jax.ShapeDtypeStruct((2, 2, outer * tower_rows, tower_width), F32),
        jax.ShapeDtypeStruct((2, GATE_STEPS * step_blocks, 2 * parts * width), F32),
        jax.ShapeDtypeStruct((6, tower_width), F32),
    ]
    size = sum(4 * math.prod(shape.shape) for shape in out_shape) // 2 + 2 * half.size
    return pl.pallas_call(
        unpack_kernel,
        grid_spec=pltpu.PrefetchScalarGridSpec(
            num_scalar_prefetch=1,
            grid=(outer // step_blocks,),
            in_specs=[pl.BlockSpec(memory_space=pltpu.VMEM)]
            + ([pl.BlockSpec((6, tower_width), lambda i, g: (0, 0))] if filled else [])
            + [pl.BlockSpec(memory_space=pl.ANY)] * (len(filled) - 1),
            out_specs=[
                pl.BlockSpec((parts, step_blocks * main_rows, width), lambda i, g: (0, i, g[0])),
                pl.BlockSpec(
                    (1, 2, step_blocks * tower_rows, tower_width), lambda i, g: (g[0], 0, i, 0)
                ),
                pl.BlockSpec(
                    (1, step_blocks, 2 * parts * width),
                    lambda i, g: (g[0], jnp.minimum(i, GATE_STEPS - 1), 0),
                ),
                pl.BlockSpec((6, tower_width), lambda i, g: (0, 0)),
            ],
        ),
        out_shape=out_shape,
        input_output_aliases={3 + i: i for i in range(len(filled) - 1)},
        cost_estimate=pl.CostEstimate(flops=half.size, bytes_accessed=size, transcendentals=0),
        compiler_params=pltpu.CompilerParams(vmem_limit_bytes=14 * 1024 * 1024),
    )(place.astype(jnp.int32).reshape(1), half.reshape(parts, outer, each, width), *filled[3:], *filled[:3])


def dispatch_kernel(ids_ref, rows_ref, out_ref, target_ref, *, experts, first_slot):
    step = pl.program_id(0)
    count = rows_ref.shape[0]
    block_experts, slots, _ = out_ref.shape

    @pl.when(step == 0)
    def _():
        ids = ids_ref[...]
        expert = lax.broadcasted_iota(jnp.int32, (experts, count), 0)
        hot = [expert == ids[c : c + 1] for c in range(2)]
        named = jnp.where(hot[0] | hot[1], 1.0, 0.0).astype(BF16)
        order = [lax.broadcasted_iota(jnp.int32, (count, count), d) for d in (0, 1)]
        before = jnp.where(order[0] < order[1], 1.0, 0.0).astype(BF16)
        earlier = jnp.dot(named, before, preferred_element_type=F32)
        for c in range(2):
            slot = jnp.sum(jnp.where(hot[c], earlier, 0.0), 0, keepdims=True).astype(jnp.int32)
            local = slot - first_slot
            inside = (local >= 0) & (local < slots)
            target_ref[c : c + 1, :] = jnp.where(inside, ids[c : c + 1] * slots + local, -1)

    block = block_experts * slots
    place = step * block + lax.broadcasted_iota(jnp.int32, (block, count), 0)
    chosen = (place == target_ref[0:1, :]) | (place == target_ref[1:2, :])
    pick = jnp.where(chosen, 1.0, 0.0).astype(BF16)
    rows = jnp.dot(pick, rows_ref[...], preferred_element_type=F32).astype(BF16)
    out_ref[...] = rows.reshape(out_ref.shape)


def dispatch(ids_by_choice, rows, experts, slots, first_slot):
    count, feature_dim = rows.shape
    block_experts = experts // 2
    return pl.pallas_call(
        functools.partial(dispatch_kernel, experts=experts, first_slot=first_slot),
        grid=(2,),
        in_specs=[
            pl.BlockSpec((2, count), lambda i: (0, 0)),
            pl.BlockSpec((count, feature_dim), lambda i: (0, 0)),
        ],
        out_specs=pl.BlockSpec((block_experts, slots, feature_dim), lambda i: (i, 0, 0)),
        out_shape=jax.ShapeDtypeStruct((experts, slots, feature_dim), BF16),
        scratch_shapes=[pltpu.VMEM((2, count), jnp.int32)],
        cost_estimate=pl.CostEstimate(
            flops=2 * experts * slots * rows.size,
            bytes_accessed=2 * rows.size + 2 * experts * slots * feature_dim,
            transcendentals=0,
        ),
        compiler_params=pltpu.CompilerParams(vmem_limit_bytes=56 * 1024 * 1024),
    )(ids_by_choice, rows)


def student_first_kernel(
    part_ref,
    kept_ref,
    experts_ref,
    gates_ref,
    tower_ref,
    pre_ref,
    logit_ref,
    experts_out_ref,
    gates_out_ref,
    tower_out_ref,
    own_ref,
    gates_own_ref,
    sems,
):
    half = kept_ref.shape[1]
    part = part_ref[0]
    own = pl.ds(pl.multiple_of(part * half, half), half)
    other = pl.ds(pl.multiple_of((1 - part) * half, half), half)
    copies = [
        pltpu.make_async_copy(experts_ref.at[own], own_ref, sems.at[0]),
        pltpu.make_async_copy(gates_ref.at[:, own], gates_own_ref, sems.at[1]),
        pltpu.make_async_copy(experts_ref.at[other], experts_out_ref, sems.at[2]),
        pltpu.make_async_copy(gates_ref.at[:, other], gates_out_ref, sems.at[3]),
        pltpu.make_async_copy(tower_ref, tower_out_ref, sems.at[4]),
    ]
    for copy in copies:
        copy.start()
    kept = kept_ref[...]
    copies[0].wait()
    pre_ref[...] = jnp.dot(kept, own_ref[...], preferred_element_type=F32)
    copies[1].wait()
    logit_ref[...] = lax.dot_general(
        kept, gates_own_ref[...], (((1,), (1,)), ((), ())), preferred_element_type=F32
    )
    for copy in copies[2:]:
        copy.wait()


def student_first(part, kept, experts_w, gates_t, tower_w):
    rows, half = kept.shape
    vmem = pl.BlockSpec(memory_space=pltpu.VMEM)
    anywhere = pl.BlockSpec(memory_space=pl.ANY)
    experts_half = (half, experts_w.shape[1])
    gates_half = (gates_t.shape[0], half)
    return pl.pallas_call(
        student_first_kernel,
        in_specs=[pl.BlockSpec(memory_space=pltpu.SMEM), vmem, anywhere, anywhere, anywhere],
        out_specs=[vmem] * 5,
        out_shape=[
            jax.ShapeDtypeStruct((rows, experts_w.shape[1]), F32),
            jax.ShapeDtypeStruct((rows, gates_t.shape[0]), F32),
            jax.ShapeDtypeStruct(experts_half, BF16),
            jax.ShapeDtypeStruct(gates_half, BF16),
            jax.ShapeDtypeStruct(tower_w.shape, BF16),
        ],
        scratch_shapes=[
            pltpu.VMEM(experts_half, BF16),
            pltpu.VMEM(gates_half, BF16),
            pltpu.SemaphoreType.DMA((5,)),
        ],
        cost_estimate=pl.CostEstimate(
            flops=rows * experts_w.size, bytes_accessed=2 * experts_w.size, transcendentals=0
        ),
        compiler_params=pltpu.CompilerParams(vmem_limit_bytes=14 * 1024 * 1024),
    )(part.reshape(1), kept, experts_w, gates_t, tower_w)


def student_kernel(
    group_ref,
    taken_ref,
    first_pre_ref,
    first_logit_ref,
    experts_ref,
    gates_ref,
    tower_in_ref,
    tower_out_ref,
    labels_ref,
    mine_ref,
    theirs_ref,
    tower_mine_ref,
    tower_theirs_ref,
    act_ref,
    slope_ref,
    *,
    loss_scale,
):
    tasks, width, tower_width = tower_in_ref.shape
    columns = gates_ref.shape[0]
    experts = columns // tasks
    group = group_ref[0]
    taken = taken_ref[...]
    across = (((1,), (1,)), ((), ()))
    down = (((0,), (0,)), ((), ()))

    logit = first_logit_ref[...] + lax.dot_general(
        taken, gates_ref[...], across, preferred_element_type=F32
    )
    sig = jax.nn.sigmoid(logit)
    task_of = [lax.broadcasted_iota(jnp.int32, (columns, columns), d) // experts for d in (0, 1)]
    same_task = jnp.where(task_of[0] == task_of[1], 1.0, 0.0)

    def task_sum(value):
        return jnp.dot(
            value, same_task, precision=lax.Precision.HIGHEST, preferred_element_type=F32
        )

    gate_sum = task_sum(sig)
    share = sig / gate_sum

    scale = math.sqrt(2.0 / math.pi)
    per_piece = 2
    for k in range(experts):
        if k % per_piece == 0:
            at = slice(k * width, (k + per_piece) * width)
            wide = first_pre_ref[:, at]
            wide += jnp.dot(taken, experts_ref[:, at], preferred_element_type=F32)
        pre = wide[:, k % per_piece * width : (k % per_piece + 1) * width]
        square = pre * pre
        tanh = jnp.tanh(scale * (pre + 0.044715 * (square * pre)))
        cdf = 0.5 * (1.0 + tanh)
        act_ref[k] = pre * cdf
        slope_ref[k] = cdf + (0.5 * scale) * pre * (1.0 - tanh * tanh) * (
            1.0 + (3 * 0.044715) * square
        )

    mix_grads, tower_in_grads = [], []
    lane = lax.broadcasted_iota(jnp.int32, share.shape, 1)
    share_grad = jnp.zeros(share.shape, F32)
    per_group = tasks // 2
    vector_rows = tower_mine_ref.shape[0] - per_group * width
    vector_row = lax.broadcasted_iota(jnp.int32, (vector_rows, tower_width), 0)
    vectors = [jnp.zeros((vector_rows, tower_width), F32)] * 2
    for t in range(tasks):
        mixture = jnp.zeros(act_ref.shape[1:], F32)
        for k in range(experts):
            column = t * experts + k
            mixture += share[:, column : column + 1] * act_ref[k]
        mixture = mixture.astype(BF16)
        tower_w = tower_in_ref[t]
        tower_pre = jnp.dot(mixture, tower_w, preferred_element_type=F32)
        tower_sig = jax.nn.sigmoid(tower_pre)
        tower_hid = tower_pre * tower_sig
        tower_vec = tower_out_ref[t : t + 1, :].astype(F32)
        task_logit = jnp.sum(tower_hid * tower_vec, 1, keepdims=True)
        mask = labels_ref[:, tasks + t : tasks + t + 1]
        error = jax.nn.sigmoid(task_logit) - labels_ref[:, t : t + 1]
        logit_grad = mask * error * loss_scale
        owner, local = t // per_group, t % per_group
        vectors[owner] = jnp.where(
            vector_row == local,
            jnp.sum(logit_grad * tower_hid, 0, keepdims=True),
            vectors[owner],
        )
        tower_grad = (
            (logit_grad * tower_vec) * tower_sig * (1.0 + tower_pre * (1.0 - tower_sig))
        ).astype(BF16)
        tower_in_grads.append(
            lax.dot_general(mixture, tower_grad, down, preferred_element_type=F32)
        )
        mix_grad = lax.dot_general(tower_grad, tower_w, across, preferred_element_type=F32)
        mix_grads.append(mix_grad)
        for k in range(experts):
            value = jnp.sum(mix_grad * act_ref[k], 1, keepdims=True)
            share_grad = jnp.where(lane == t * experts + k, value, share_grad)

    low_group = group == 0
    for local in range(per_group):
        at = slice(local * width, (local + 1) * width)
        low, high = tower_in_grads[local], tower_in_grads[local + per_group]
        tower_mine_ref[at] = jnp.where(low_group, low, high).astype(BF16)
        tower_theirs_ref[at] = jnp.where(low_group, high, low).astype(BF16)
    tower_mine_ref[per_group * width :] = jnp.where(low_group, vectors[0], vectors[1]).astype(BF16)
    tower_theirs_ref[per_group * width :] = jnp.where(low_group, vectors[1], vectors[0]).astype(
        BF16
    )

    def pre_grad(k):
        act_grad = jnp.zeros(act_ref.shape[1:], F32)
        for t in range(tasks):
            column = t * experts + k
            act_grad += share[:, column : column + 1] * mix_grads[t]
        return act_grad * slope_ref[k]

    for k in range(experts // 2):
        at = slice(k * width, (k + 1) * width)
        low, high = pre_grad(k), pre_grad(k + experts // 2)
        mine_ref[:, at] = jnp.where(low_group, low, high).astype(BF16)
        theirs_ref[:, at] = jnp.where(low_group, high, low).astype(BF16)

    sig_grad = (share_grad - task_sum(share * share_grad)) / gate_sum
    gate_grad = (sig_grad * sig * (1.0 - sig)).astype(BF16)
    end = experts // 2 * width
    lanes = mine_ref.shape[1] - end
    source = lax.broadcasted_iota(jnp.int32, (columns, lanes), 0)
    lane_at = lax.broadcasted_iota(jnp.int32, (columns, lanes), 1)
    for ref, owner in ((mine_ref, group), (theirs_ref, 1 - group)):
        wanted = (source == lane_at + owner * (columns // 2)) & (lane_at < columns // 2)
        move = jnp.where(wanted, 1.0, 0.0).astype(BF16)
        ref[:, end:] = jnp.dot(gate_grad, move, preferred_element_type=F32).astype(BF16)


def student_grads(group, taken, first_part, tower_v, labels, loss_scale):
    pre, _, _, _, tower_w = first_part
    rows, columns = pre.shape
    tasks, width, tower_width = tower_w.shape
    experts = columns // width
    vmem = pl.BlockSpec(memory_space=pltpu.VMEM)
    factor = jax.ShapeDtypeStruct((rows, columns // 2 + 128), BF16)
    tower = jax.ShapeDtypeStruct((tasks // 2 * width + 16, tower_width), BF16)
    return pl.pallas_call(
        functools.partial(student_kernel, loss_scale=loss_scale),
        in_specs=[pl.BlockSpec(memory_space=pltpu.SMEM)] + [vmem] * 8,
        out_specs=[vmem] * 4,
        out_shape=[factor, factor, tower, tower],
        scratch_shapes=[pltpu.VMEM((experts, rows, width), F32)] * 2,
        cost_estimate=pl.CostEstimate(
            flops=rows * taken.shape[1] * columns, bytes_accessed=4 * pre.size, transcendentals=0
        ),
        compiler_params=pltpu.CompilerParams(vmem_limit_bytes=14 * 1024 * 1024),
    )(group.reshape(1), taken, *first_part, tower_v, labels)


def pack_kernel(
    own_rows_ref,
    other_rows_ref,
    mine_ref,
    from_part_ref,
    theirs_ref,
    from_far_ref,
    tower_mine_ref,
    tower_theirs_ref,
    out_ref,
    rows_ref,
    factor_ref,
    tower_ref,
    block_ref,
):
    blocks, each, width = out_ref.shape
    count = mine_ref.shape[0]
    main_rows = each - 8
    down = (((0,), (0,)), ((), ()))
    rows_ref[: 2 * count] = own_rows_ref[...]
    rows_ref[2 * count :] = other_rows_ref[...]
    factor_ref[:count] = mine_ref[...]
    factor_ref[count : 2 * count] = from_part_ref[...]
    factor_ref[2 * count : 3 * count] = theirs_ref[...]
    factor_ref[3 * count :] = from_far_ref[...]
    tower_ref[...] = tower_mine_ref[...].astype(F32) + tower_theirs_ref[...].astype(F32)
    tower_rows = tower_ref.shape[0] - 16
    window = tower_rows // 2 // blocks
    gates = lax.dot_general(
        factor_ref[:, width:], rows_ref[...], down, preferred_element_type=F32
    )
    gate_count = GATE_STEPS * 8
    per_step = 8
    for step in range(blocks // per_step):
        at = step * per_step * main_rows
        main = lax.dot_general(
            rows_ref[:, at : at + per_step * main_rows],
            factor_ref[:, :width],
            down,
            preferred_element_type=F32,
        )
        for local in range(per_step):
            block = step * per_step + local
            block_ref[:main_rows] = main[local * main_rows : (local + 1) * main_rows]
            if block < gate_count:
                block_ref[main_rows : main_rows + 1] = gates[block : block + 1, :width]
                block_ref[main_rows + 1 : main_rows + 2] = gates[block : block + 1, width:]
            else:
                block_ref[main_rows : main_rows + 2] = jnp.zeros((2, width), F32)
            if block == gate_count:
                vectors = tower_ref[tower_rows:]
                half = width // 2
                block_ref[main_rows : main_rows + 1, :half] = vectors[0:1]
                block_ref[main_rows : main_rows + 1, half:] = vectors[1:2]
                block_ref[main_rows + 1 : main_rows + 2, :half] = vectors[2:3]
            low = tower_ref[block * window : (block + 1) * window]
            high = tower_ref[tower_rows // 2 + block * window : tower_rows // 2 + (block + 1) * window]
            block_ref[main_rows + 2 : main_rows + 2 + window, : width // 2] = low
            block_ref[main_rows + 2 : main_rows + 2 + window, width // 2 :] = high
            out_ref[block] = block_ref[...].astype(BF16)


def pack(own_rows, other_rows, mine, from_part, theirs, from_far, tower_mine, tower_theirs, blocks):
    count, features = own_rows.shape
    width = features // 2
    each = features // blocks + 8
    vmem = pl.BlockSpec(memory_space=pltpu.VMEM)
    return pl.pallas_call(
        pack_kernel,
        in_specs=[vmem] * 8,
        out_specs=vmem,
        out_shape=jax.ShapeDtypeStruct((blocks, each, width), BF16),
        scratch_shapes=[
            pltpu.VMEM((2 * count, features), BF16),
            pltpu.VMEM((2 * count, mine.shape[1]), BF16),
            pltpu.VMEM(tower_mine.shape, F32),
            pltpu.VMEM((each, width), F32),
        ],
        cost_estimate=pl.CostEstimate(
            flops=4 * count * features * width,
            bytes_accessed=2 * blocks * each * width,
            transcendentals=0,
        ),
        compiler_params=pltpu.CompilerParams(vmem_limit_bytes=14 * 1024 * 1024),
    )(own_rows, other_rows, mine, from_part, theirs, from_far, tower_mine, tower_theirs)


def on_device(
    teacher_rows,
    expert_ids,
    router,
    teacher_up,
    teacher_down,
    student_experts,
    student_gates,
    tower_in,
    tower_out,
    soft_labels,
    label_masks,
):
    rows_dev, feature_dim = teacher_rows.shape
    expert_total = lax.axis_size("ep")
    width_parts = lax.axis_size("mp")
    group_index = lax.axis_index("grp")
    chips = expert_total * width_parts
    capacity = 4 * rows_dev // expert_total
    chunk_slots = capacity // SLOT_CHUNKS

    labels = swap(jnp.concatenate([soft_labels, label_masks.astype(F32)], 1), "grp")

    experts = jnp.arange(expert_total, dtype=jnp.int32)
    hot = [(expert_ids[:, c : c + 1] == experts[None, :]) for c in range(2)]
    named = (hot[0] | hot[1]).astype(BF16)
    sample = jnp.arange(rows_dev, dtype=jnp.int32)
    before = (sample[None, :] < sample[:, None]).astype(BF16)
    earlier = jnp.dot(before, named, preferred_element_type=F32)
    slots = [jnp.sum(jnp.where(h, earlier, 0.0), 1, keepdims=True).astype(jnp.int32) for h in hot]

    def places(chunk):
        found = []
        for c in range(2):
            local = slots[c] - chunk * chunk_slots
            inside = (local >= 0) & (local < chunk_slots)
            found.append(jnp.where(inside, expert_ids[:, c : c + 1] * chunk_slots + local, -1))
        return found

    targets = [places(chunk) for chunk in range(SLOT_CHUNKS)]

    received = []
    for chunk in range(SLOT_CHUNKS):
        outgoing = dispatch(
            expert_ids.T, teacher_rows, expert_total, chunk_slots, chunk * chunk_slots
        )
        received.append(lax.all_to_all(outgoing, "ep", split_axis=0, concat_axis=0, tiled=True))

    logits = jnp.dot(teacher_rows, router, preferred_element_type=F32)
    chosen = [jnp.sum(jnp.where(h, logits, 0.0), 1, keepdims=True) for h in hot]
    sigs = [jax.nn.sigmoid(v) for v in chosen]
    weights = [v / (sigs[0] + sigs[1]) for v in sigs]

    up_proj = teacher_up[0]
    down_proj = teacher_down[0]
    part = lax.axis_index("mp")
    half_width = feature_dim // width_parts
    mixed = jnp.zeros((rows_dev, half_width), F32)
    wide_lane = jnp.arange(chips * chunk_slots, dtype=jnp.int32)[None, :]
    wide_place = wide_lane % (expert_total * chunk_slots)
    for chunk in range(SLOT_CHUNKS):
        rows_in = received[chunk].reshape(expert_total * chunk_slots, feature_dim)
        inner = jax.nn.gelu(jnp.dot(rows_in, up_proj, preferred_element_type=F32)).astype(BF16)
        partial = jnp.dot(inner, down_proj, preferred_element_type=F32).astype(BF16)
        outgoing = partial.reshape(expert_total, chunk_slots, width_parts, half_width)
        outgoing = outgoing.transpose(2, 0, 1, 3).reshape(chips, chunk_slots, half_width)
        returned = lax.all_to_all(outgoing, CHIPS, split_axis=0, concat_axis=0, tiled=True)
        returned = returned.reshape(chips * chunk_slots, half_width)
        first, second = targets[chunk]
        share = jnp.where(wide_place == first, weights[0], 0.0) + jnp.where(
            wide_place == second, weights[1], 0.0
        )
        mixed = mixed + jnp.dot(share.astype(BF16), returned, preferred_element_type=F32)
    mixed = mixed.astype(BF16)

    half_rows = rows_dev // width_parts
    kept = lax.dynamic_slice_in_dim(mixed, part * half_rows, half_rows, 0)
    given = lax.dynamic_slice_in_dim(mixed, (1 - part) * half_rows, half_rows, 0)
    taken = swap(given, "mp")
    first_part = student_first(part, kept, student_experts, student_gates.T, tower_in)
    sample_total = rows_dev * lax.axis_size("grp") * expert_total
    mine, theirs, tower_mine, tower_theirs = student_grads(
        group_index, taken, first_part, tower_out, labels, 1.0 / math.sqrt(sample_total)
    )
    from_part = swap(mine, "mp")
    from_far = lax.ppermute(theirs, ("grp", "mp"), [(i, 3 - i) for i in range(4)])
    theirs = swap(theirs, "grp")
    tower_theirs = swap(tower_theirs, "grp")
    own_kept, own_given, mine = lax.optimization_barrier((kept, given, mine))
    both = jnp.concatenate([own_kept, own_given], 0)
    other_both = swap(both, "grp")
    packed = pack(
        both, other_both, mine, from_part, theirs, from_far, tower_mine, tower_theirs, expert_total
    )

    parts = lax.all_to_all(packed, "ep", split_axis=0, concat_axis=0, tiled=True)
    total = jnp.sum(parts.astype(F32), 0).astype(BF16)
    spread = jnp.broadcast_to(total[None], (chips,) + total.shape)
    own_half = lax.all_to_all(spread, CHIPS, split_axis=0, concat_axis=0, tiled=True)
    other_half = swap(own_half, "grp")
    filled = unpack(own_half, group_index, chips, width_parts, ())
    main, tower, gates, vector = unpack(other_half, 1 - group_index, chips, width_parts, filled)
    return (
        main.reshape(student_experts.shape),
        gates.reshape(-1, feature_dim).T,
        tower.reshape(tower_in.shape),
        vector,
    )


def solution(mesh):
    return jax.shard_map(
        on_device,
        mesh=mesh,
        in_specs=(
            P(("grp", "ep"), None),
            P(("grp", "ep"), None),
            P(),
            P("ep", None, "mp"),
            P("ep", "mp", None),
            P(),
            P(),
            P(),
            P(),
            P(("grp", "ep", "mp"), None),
            P(("grp", "ep", "mp"), None),
        ),
        out_specs=(P(), P(), P(), P()),
        check_vma=False,
    )
```
